512 devices in a mesh: member: 8 (over z_hi, core), lat: 64 (over z_lo, x, y).
Axes of the slice: x: 4, y: 8, z: 8 (z_hi: 4, z_lo: 2; z = z_hi * 2 + z_lo), core: 2. Of those that a mesh axis runs over, the one named last changes fastest.
Arguments:
- members: float32 [8, 16, 512, 1440], P('member', None, 'lat'), may hold values from 0.1 to 160, as said below
- conductivity: float32 [16, 512, 1440], P(None, 'lat'), may hold values from 0.1 to 1
- weights: float32 [8], P('member'), may hold values from 0.25 to 4
Outputs:
- barycenter: float32 [16, 512, 1440], P('member', 'lat')
The draws below stay inside these ranges and needn't reach their ends.
Inputs may be any that keep to these rules, and one draw needn't show every extreme that they name: `members`: positive humidity densities.
All inputs are finite; a program needn't handle non-finite values.
Results may differ from the reference program's by a relative error of at most 0.00002.
Values sent between devices are 32-bit elements; how exact they have to be, the bound alone decides.
A program may use at most 64 MiB of HBM per device.

```python
import math
import jax
import jax.numpy as jnp
from jax import lax

LEV = 16
LON = 1440
PASSES = 3
MEMBERS = 8
LAT = 512


def draw_members(key, part):
    key = jax.random.fold_in(key, 11)
    shape = (MEMBERS, LEV, LAT, LON)
    rows = jnp.arange(LAT, dtype=jnp.float32)
    profile = 1.0 + 2.0 * rows / max(LAT - 1, 1)
    levels = jnp.arange(LEV, dtype=jnp.float32)
    level_rise = 1.0 + 3.0 * levels / max(LEV - 1, 1)
    roughness = jax.random.truncated_normal(key, -3.0, 3.0, shape, jnp.float32)
    values = jnp.exp(0.5 * roughness) * profile[None, None, :, None]
    values = values * level_rise[None, :, None, None]
    return values.astype(jnp.float32)


def steps_of(rng, extent, cuts, smallest, top_value):
    factor_of, own = 1.0, jax.random.fold_in(rng, 6)
    for axis_at, shards_of in cuts:
        heights = jnp.exp(jax.random.uniform(jax.random.fold_in(own, axis_at), (shards_of,), jnp.float32, smallest / len(cuts), top_value / len(cuts)))
        factor_of = factor_of * jnp.repeat(heights, extent[axis_at] // shards_of).reshape([-1 if axis == axis_at else 1 for axis in range(len(extent))])
    return factor_of


def setup_inputs(seed: int = 0) -> dict:
    arg_keys = jax.random.split(jax.random.key(seed), 4)
    return {
        "members": draw_members(jax.random.fold_in(arg_keys[3], 71), 0),
        "conductivity": jnp.clip(jnp.exp(math.log(1.0) - 2.3025851 * jax.random.uniform(arg_keys[1], (LEV, LAT, LON), jnp.float32) ** steps_of(arg_keys[1], (LEV, LAT, LON), ((1, 64),), -0.2, 0.2)), 0.1, 1.0),
        "weights": jnp.clip(jnp.exp(math.log(4.0) - 2.7725887 * jax.random.uniform(arg_keys[2], (MEMBERS,), jnp.float32) ** steps_of(arg_keys[2], (MEMBERS,), ((0, 8),), -0.2, 0.2)), 0.25, 4.0),
    }


step_size = 0.16

def build_faces(cond_padded):
    lat_face = jnp.sqrt(cond_padded[:, 1:, :] * cond_padded[:, :-1, :])
    lon_face = jnp.sqrt(cond_padded * jnp.roll(cond_padded, -1, axis=-1))
    lev_face = jnp.sqrt(cond_padded[1:] * cond_padded[:-1])
    return (lat_face, lon_face, lev_face)

def heat_pass(padded, first_row, face_tables):
    lat_face, lon_face, lev_face = face_tables
    row_count = padded.shape[-2]
    centre = padded[..., 1:-1, :]
    north_face = lat_face[:, first_row + 1:first_row + row_count - 1, :]
    south_face = lat_face[:, first_row:first_row + row_count - 2, :]
    inflow = north_face * (padded[..., 2:, :] - centre) + south_face * (padded[..., :-2, :] - centre)
    zonal_face = lon_face[:, first_row + 1:first_row + row_count - 1, :]
    inflow = inflow + zonal_face * (jnp.roll(centre, -1, axis=-1) - centre)
    inflow = inflow + jnp.roll(zonal_face, 1, axis=-1) * (jnp.roll(centre, 1, axis=-1) - centre)
    vertical_face = lev_face[:, first_row + 1:first_row + row_count - 1, :]
    level_flux = vertical_face * (centre[..., 1:, :, :] - centre[..., :-1, :, :])
    boundary = jnp.zeros_like(level_flux[..., :1, :, :])
    inflow = inflow + jnp.concatenate([level_flux, boundary], axis=-3) - jnp.concatenate([boundary, level_flux], axis=-3)
    return centre + step_size * inflow

def reference(members, conductivity, weights):
    member_weight = weights / jnp.sum(weights)
    face_tables = build_faces(jnp.pad(conductivity, ((0, 0), (1, 1), (0, 0))))

    def kernel(heated):
        for pass_index in range(PASSES):
            heated = heat_pass(jnp.pad(heated, ((0, 0), (1, 1), (0, 0))), 0, face_tables)
        return heated

    def first_step(running, current):
        density, member_share = current
        marginal = kernel(density)
        return (running + member_share * jnp.log(marginal), marginal)
    log_sum, marginals = lax.scan(first_step, jnp.zeros_like(conductivity), (members, member_weight))
    first = jnp.exp(log_sum)

    def second_step(running, current):
        density, marginal, member_share = current
        scaling = first / marginal
        renewed = scaling * kernel(density / kernel(scaling))
        return (running + member_share * jnp.log(renewed), None)
    log_sum, unused = lax.scan(second_step, jnp.zeros_like(conductivity), (members, marginals, member_weight))
    second = jnp.exp(log_sum)
    cell_count = second.size
    return second * (cell_count / jnp.sum(second))
```

```python
import functools

import jax
import jax.numpy as jnp
from jax import lax
from jax.experimental import pallas as pl
from jax.experimental.pallas import tpu as pltpu
from jax.sharding import PartitionSpec as P

MESH = pl.DeviceIdType.MESH
STEP = 0.16
PASSES = 3
LEV, ROWS, LON = 16, 8, 1440
HALF = LEV // 2
CHUNKS = 4
COLS = LON // CHUNKS
GHOST = 12
LANES = COLS + 2 * GHOST
TILES = LANES // 128
HALO = 3 * PASSES
ALL = ROWS + 2 * HALO
OWN = HALO
MARGIN = 2 * PASSES
INNER = ROWS + 2 * MARGIN


def lane_tiles(ref, lev):
    def tile(index):
        if index < 11:
            return ref[lev, :, pl.ds(128 * index, 128)]
        return pltpu.roll(ref[lev, :, pl.ds(LON - 128, 128)], 32, 1)

    return tile


def lane_chunk(tiles, part):
    lane = lax.broadcasted_iota(jnp.int32, (ROWS, 128), 1)
    if part == 0:
        window = [pltpu.roll(tiles(11), 96, 1), tiles(0), tiles(1), tiles(2)]
    elif part == CHUNKS - 1:
        last = jnp.where(lane < 32, tiles(11), pltpu.roll(tiles(0), 32, 1))
        window = [tiles(8), tiles(9), tiles(10), last]
    else:
        first = (COLS * part - GHOST) // 128
        window = [tiles(first + i) for i in range(4)]
    shift = (COLS * part - GHOST) % 128
    return pltpu.roll(jnp.concatenate(window, axis=1), 512 - shift, 1)[:, :LANES]


def join_chunks(chunks):
    lane = lax.broadcasted_iota(jnp.int32, (ROWS, 128), 1)
    windows, starts = [], []
    for part, chunk in enumerate(chunks):
        start = COLS * part
        wide = jnp.concatenate([chunk, jnp.zeros((ROWS, 128), jnp.float32)], axis=1)
        wide = pltpu.roll(wide, (start % 128 - GHOST) % 512, 1)
        windows.append([wide[:, 128 * i : 128 * (i + 1)] for i in range(4)])
        starts.append(start)
    tiles = []
    for index in range(12):
        tile = None
        for part, start in enumerate(starts):
            at = index - start // 128
            if 0 <= at < 4 and start < 128 * (index + 1) and start + COLS > 128 * index:
                piece = windows[part][at]
                tile = piece if tile is None else jnp.where(lane < start % 128, tile, piece)
        tiles.append(tile)
    return tiles


def kernel(
    members, conductivity, weights, out, scale,
    xm, xc, sends, slabs, cond, cond_far, table_s, table_d, table_g, start, buf_a, buf_b,
    logs, logs_other, final, final_other, shares, gathered, weight_own, weight_in, weight_sum, weight_other, mass, column_in, plane_in,
    load_sem, local_sem, z_send, z_recv, w_send, w_recv, c_send, c_recv, y_send, y_recv, f_send, f_recv,
    s_send, s_recv, g_send, g_recv, t_send, t_recv, p_send, p_recv,
):
    me = lax.axis_index("member")
    lat = lax.axis_index("lat")
    zone, core = me // 2, lax.rem(me, 2)
    lat_count = lax.axis_size("lat")

    def zone_peer(k):
        return {"member": lax.rem(zone + k, CHUNKS) * 2 + core}

    def lat_peer(k):
        return {"lat": lax.rem(lat + k + lat_count, lat_count)}

    sibling = {"member": me + 1 - 2 * core}

    def column_peer(k):
        place = lax.rem(2 * zone + lat // 32 + k, 8)
        return {"member": place // 2 * 2 + core, "lat": lax.rem(place, 2) * 32 + lax.rem(lat, 32)}

    def plane_peer(k):
        return {"lat": lat // 32 * 32 + lax.rem(lat + k, 32)}

    load_c = pltpu.make_async_copy(conductivity, xc, load_sem.at[0])
    load_m = pltpu.make_async_copy(members.at[0], xm, load_sem.at[1])
    load_c.start()
    load_m.start()

    barrier = pltpu.get_barrier_semaphore()
    partners = [lat_peer(k) for k in (1, -1, 2, -2)] + [sibling] + [column_peer(k) for k in range(1, 8)]
    for partner in partners:
        pl.semaphore_signal(barrier, inc=1, device_id=partner, device_id_type=MESH)

    def greet(k, carry):
        pl.semaphore_signal(barrier, inc=1, device_id=plane_peer(k), device_id_type=MESH)
        return carry

    lax.fori_loop(1, 32, greet, 0)

    def remote(src, dst, send, recv, target):
        return pltpu.make_async_remote_copy(
            src_ref=src, dst_ref=dst, send_sem=send, recv_sem=recv, device_id=target, device_id_type=MESH
        )

    load_c.wait()
    for part in range(CHUNKS):

        @pl.when(zone == part)
        def _(part=part):
            for lev in range(LEV):
                place = lev if lev < HALF else HALF + LEV - 1 - lev
                tiles = lane_tiles(xc, lev)
                cond[1, place] = lane_chunk(tiles, part)

    weight_own[...] = jnp.full((8, 128), weights[0], jnp.float32)
    load_m.wait()
    for lev in range(LEV):
        half, place = (0, lev) if lev < HALF else (1, LEV - 1 - lev)
        tiles = lane_tiles(xm, lev)
        for part in range(CHUNKS):
            chunk = lane_chunk(tiles, part)
            for t in range(TILES):
                sends[part, t, place, pl.ds(8 * half, 8), :] = chunk[:, 128 * t : 128 * (t + 1)]

    pl.semaphore_wait(barrier, len(partners) + 31)

    def block(b):
        return pl.ds(pl.multiple_of(16 * b, 16), 16)

    zone_copies = {
        k: remote(
            sends.at[lax.rem(zone + k, CHUNKS)], slabs.at[1, :, :, block(zone), :], z_send.at[k - 1], z_recv.at[k - 1],
            zone_peer(k),
        )
        for k in (1, 3, 2)
    }
    weight_copies = [
        remote(weight_own, weight_in.at[k - 1], w_send.at[k - 1], w_recv.at[k - 1], zone_peer(k)) for k in (1, 2, 3)
    ]
    cond_copies = [
        remote(cond.at[1], cond.at[0], c_send.at[0], c_recv.at[0], lat_peer(1)),
        remote(cond.at[1], cond.at[2], c_send.at[1], c_recv.at[1], lat_peer(-1)),
        remote(cond.at[1, :, pl.ds(7, 1), :], cond_far.at[0, :, pl.ds(0, 1), :], c_send.at[2], c_recv.at[2], lat_peer(2)),
        remote(cond.at[1, :, pl.ds(0, 1), :], cond_far.at[1, :, pl.ds(0, 1), :], c_send.at[3], c_recv.at[3], lat_peer(-2)),
    ]
    for k in (1, 3, 2):
        zone_copies[k].start()
    for copy in cond_copies:
        copy.start()
    for copy in weight_copies:
        copy.start()
    mine = pltpu.make_async_copy(sends.at[zone], slabs.at[1, :, :, block(zone), :], local_sem.at[0])
    mine.start()

    def forward(k):
        source = lax.rem(zone - k + CHUNKS, CHUNKS)
        part = slabs.at[1, :, :, block(source), :]
        return [
            remote(part, slabs.at[0, :, :, block(source), :], y_send.at[k, 0], y_recv.at[k, 0], lat_peer(1)),
            remote(part, slabs.at[2, :, :, block(source), :], y_send.at[k, 1], y_recv.at[k, 1], lat_peer(-1)),
        ]

    row_copies = []
    mine.wait()
    for copy in forward(0):
        copy.start()
        row_copies.append(copy)

    sub = lax.broadcasted_iota(jnp.int32, (8, LANES), 0)
    even = sub % 2 == 0

    def spread(low, high):
        return jnp.where(even, jnp.broadcast_to(low, (8, LANES)), jnp.broadcast_to(high, (8, LANES)))

    def swap_halves(value):
        return jnp.where(even, pltpu.roll(value, 7, 0), pltpu.roll(value, 1, 0))

    def around(src, row):
        centre = [src[row, place] for place in range(HALF)]
        sums = []
        for place in range(HALF):
            value = centre[place]
            total = src[row - 1, place] + src[row + 1, place]
            total = total + (pltpu.roll(value, 1, 1) + pltpu.roll(value, LANES - 1, 1))
            if place > 0:
                total = total + centre[place - 1]
            total = total + (centre[place + 1] if place < HALF - 1 else swap_halves(value))
            sums.append(total)
        return centre, sums

    for copy in cond_copies:
        copy.wait()
    inside_low = jnp.where(lat == 0, 0.0, 1.0)
    inside_high = jnp.where(lat == lat_count - 1, 0.0, 1.0)
    far_low = jnp.where(lat <= 1, 0.0, 1.0)
    far_high = jnp.where(lat >= lat_count - 2, 0.0, 1.0)

    def root_rows(slab, first, inside):
        def body(row, carry):
            for place in range(HALF):
                low = cond[slab, place, pl.ds(row, 1), :]
                high = cond[slab, HALF + place, pl.ds(row, 1), :]
                table_s[first + row, place] = jnp.sqrt(spread(low, high)) * inside
            return carry

        lax.fori_loop(0, ROWS, body, 0)

    root_rows(0, OWN - ROWS, inside_low)
    root_rows(1, OWN, 1.0)
    root_rows(2, OWN + ROWS, inside_high)
    for side, row, inside in ((0, 0, far_low), (1, ALL - 1, far_high)):
        for place in range(HALF):
            low = cond_far[side, place, pl.ds(0, 1), :]
            high = cond_far[side, HALF + place, pl.ds(0, 1), :]
            table_s[row, place] = jnp.sqrt(spread(low, high)) * inside

    def table_row(row, carry):
        centre, sums = around(table_s, row)
        for place in range(HALF):
            table_d[row, place] = 1.0 - STEP * (centre[place] * sums[place])
            table_g[row, place] = STEP * (centre[place] * centre[place])
        return carry

    lax.fori_loop(1, ALL - 1, table_row, 0)

    for k in (1, 3, 2):
        zone_copies[k].wait_recv()
        for copy in forward(k):
            copy.start()
            row_copies.append(copy)

    def rows_across(ref, place, row):
        parts = [ref[t, place, pl.ds(row, 8, stride=8), :] for t in range(TILES)]
        return jnp.concatenate(parts, axis=1)

    def start_rows(slab, first):
        def body(row, carry):
            for place in range(HALF):
                value = rows_across(slabs.at[slab], place, row)
                start[first + row, place] = value * table_s[first + row, place]
            return carry

        lax.fori_loop(0, ROWS, body, 0)

    start_rows(1, OWN)
    far_copies = [
        remote(start.at[OWN + ROWS - 1], start.at[0], f_send.at[0], f_recv.at[0], lat_peer(2)),
        remote(start.at[OWN], start.at[ALL - 1], f_send.at[1], f_recv.at[1], lat_peer(-2)),
    ]
    for copy in far_copies:
        copy.start()
    for copy in weight_copies:
        copy.wait()
    group = lax.broadcasted_iota(jnp.int32, (8, 128), 0) // 2
    weight = jnp.zeros((8, 128), jnp.float32)
    total_weight = weight_own[...]
    for k in range(CHUNKS):
        value = weight_own[...] if k == 0 else weight_in[k - 1]
        weight = jnp.where(group == lax.rem(zone - k + CHUNKS, CHUNKS), value, weight)
        if k > 0:
            total_weight = total_weight + value
    weight_sum[...] = total_weight
    weight = jnp.concatenate([weight] * 3, axis=1)

    for copy in row_copies:
        copy.wait_recv()
    start_rows(0, OWN - ROWS)
    start_rows(2, OWN + ROWS)
    for copy in far_copies:
        copy.wait_recv()
    for row, inside in ((0, far_low), (ALL - 1, far_high)):
        for place in range(HALF):
            start[row, place] = start[row, place] * inside

    def heat(src, dst, low, high):
        def body(row, carry):
            centre, sums = around(src, row)
            for place in range(HALF):
                dst[row, place] = table_d[row, place] * centre[place] + table_g[row, place] * sums[place]
            return carry

        lax.fori_loop(low, high, body, 0)

    def guarded(value):
        return jnp.where(value > 0.0, value, 1.0)

    def fold(a, b, c, d):
        upper = sub >= 4
        odd_pair = (sub // 2) % 2 == 1

        def halves(x, y):
            return jnp.where(upper, y, x) + pltpu.roll(jnp.where(upper, x, y), 4, 0)

        x, y = halves(a, c), halves(b, d)
        other = jnp.where(odd_pair, pltpu.roll(y, 2, 0), pltpu.roll(x, 6, 0))
        return jnp.where(odd_pair, y, x) + other

    def log_sums(src, row):
        terms = [weight * jnp.log(guarded(src[row, place])) for place in range(HALF)]
        return [fold(*terms[4 * q : 4 * q + 4]) for q in range(2)]

    heat(start, buf_a, 1, ALL - 1)
    heat(buf_a, buf_b, 2, ALL - 2)
    heat(buf_b, buf_a, 3, ALL - 3)

    def first_logs(i, carry):
        for q, value in enumerate(log_sums(buf_a, i + PASSES)):
            logs[i, q] = value
        return carry

    lax.fori_loop(0, INNER, first_logs, 0)
    sibling_copies = [
        remote(logs, logs_other, s_send.at[0], s_recv.at[0], sibling),
        remote(weight_sum, weight_other, s_send.at[1], s_recv.at[1], sibling),
    ]
    for copy in sibling_copies:
        copy.start()
    for copy in sibling_copies:
        copy.wait()
    inverse = 1.0 / (weight_sum[...] + weight_other[...])
    inverse = jnp.concatenate([inverse] * 3, axis=1)

    def rescale(i, carry):
        for q in range(2):
            logs[i, q] = jnp.exp((logs[i, q] + logs_other[i, q]) * inverse)
        row = i + PASSES
        for place in range(HALF):
            q, j = place // 4, place % 4
            power = spread(logs[i, q, pl.ds(2 * j, 1), :], logs[i, q, pl.ds(2 * j + 1, 1), :])
            buf_b[row, place] = table_s[row, place] * power / guarded(buf_a[row, place])
        return carry

    lax.fori_loop(0, INNER, rescale, 0)
    heat(buf_b, buf_a, 4, ALL - 4)
    heat(buf_a, buf_b, 5, ALL - 5)
    heat(buf_b, buf_a, 6, ALL - 6)

    def ratio(row, carry):
        for place in range(HALF):
            buf_b[row, place] = start[row, place] * table_s[row, place] / guarded(buf_a[row, place])
        return carry

    lax.fori_loop(6, ALL - 6, ratio, 0)
    heat(buf_b, buf_a, 7, ALL - 7)
    heat(buf_a, buf_b, 8, ALL - 8)
    heat(buf_b, buf_a, 9, ALL - 9)

    def second_logs(i, carry):
        for q, value in enumerate(log_sums(buf_a, i + OWN)):
            for t in range(TILES):
                final[t, q, pl.ds(pl.multiple_of(8 * i, 8), 8), :] = value[:, 128 * t : 128 * (t + 1)]
        return carry

    lax.fori_loop(0, ROWS, second_logs, 0)
    final_copy = remote(final, final_other, s_send.at[2], s_recv.at[2], sibling)
    final_copy.start()
    final_copy.wait()
    lane = lax.broadcasted_iota(jnp.int32, (ROWS, LANES), 1)
    valid = (lane >= GHOST) & (lane < GHOST + COLS)
    total = jnp.zeros((ROWS, LANES), jnp.float32)
    for lev in range(LEV):
        half, place = (0, lev) if lev < HALF else (1, LEV - 1 - lev)
        at = (place // 4, 2 * (place % 4) + half)
        value = jnp.exp((rows_across(final, *at) + rows_across(final_other, *at)) * inverse)
        value = value * lax.rsqrt(cond[1, HALF * half + place])
        total = total + jnp.where(valid, value, 0.0)
        shares[lev // 4, lev // 2 % 2, lev % 2] = value
    summed = total[:, :128] + total[:, 128:256] + total[:, 256:]

    mass[0] = summed
    column_copies = [
        remote(mass.at[0], column_in.at[k - 1], t_send.at[k - 1], t_recv.at[k - 1], column_peer(k)) for k in range(1, 8)
    ]
    for copy in column_copies:
        copy.start()
    share_copies = [
        remote(
            shares.at[lax.rem(zone + k, CHUNKS), core], gathered.at[zone], g_send.at[k - 1], g_recv.at[k - 1],
            zone_peer(k),
        )
        for k in (1, 2, 3)
    ]
    for copy in share_copies:
        copy.start()
    gathered[zone] = shares[zone, core]
    for k, copy in enumerate(column_copies):
        copy.wait()
        summed = summed + column_in[k]

    mass[1] = summed

    def plane_copy(k):
        return remote(mass.at[1], plane_in.at[k - 1], p_send.at[k - 1], p_recv.at[k - 1], plane_peer(k))

    def send_plane(k, carry):
        plane_copy(k).start()
        return carry

    lax.fori_loop(1, 32, send_plane, 0)
    for copy in share_copies:
        copy.wait()
    for i in range(2):
        for index, tile in enumerate(join_chunks([gathered[part, i] for part in range(CHUNKS)])):
            if index < 11:
                out[i, :, pl.ds(128 * index, 128)] = tile
            else:
                out[i, :, pl.ds(128 * index, 32)] = tile[:, :32]

    def take_plane(k, value):
        plane_copy(k).wait()
        return value + plane_in[k - 1]

    summed = lax.fori_loop(1, 32, take_plane, summed)
    cells = LEV * ROWS * lat_count * LON
    scale[...] = jnp.full((8, 128), cells / jnp.sum(summed), jnp.float32)

    for k in (1, 2, 3):
        zone_copies[k].wait_send()
    for copy in row_copies + far_copies:
        copy.wait_send()


def local(members, conductivity, weights):
    vmem = functools.partial(pltpu.VMEM, dtype=jnp.float32)
    dma = pltpu.SemaphoreType.DMA
    field = (ALL, HALF, 8, LANES)
    value, scale = pl.pallas_call(
        kernel,
        name="barycenter",
        out_shape=[
            jax.ShapeDtypeStruct((2, ROWS, LON), jnp.float32),
            jax.ShapeDtypeStruct((8, 128), jnp.float32),
        ],
        in_specs=[
            pl.BlockSpec(memory_space=pl.ANY),
            pl.BlockSpec(memory_space=pl.ANY),
            pl.BlockSpec(memory_space=pltpu.SMEM),
        ],
        out_specs=[pl.BlockSpec(memory_space=pltpu.VMEM)] * 2,
        scratch_shapes=[
            vmem((LEV, ROWS, LON)),
            vmem((LEV, ROWS, LON)),
            vmem((CHUNKS, TILES, HALF, 16, 128)),
            vmem((3, TILES, HALF, 64, 128)),
            vmem((3, LEV, ROWS, LANES)),
            vmem((2, LEV, ROWS, LANES)),
            vmem(field), vmem(field), vmem(field), vmem(field), vmem(field), vmem(field),
            vmem((INNER, 2, 8, LANES)),
            vmem((INNER, 2, 8, LANES)),
            vmem((TILES, 2, 64, 128)),
            vmem((TILES, 2, 64, 128)),
            vmem((CHUNKS, 2, 2, ROWS, LANES)),
            vmem((CHUNKS, 2, ROWS, LANES)),
            vmem((8, 128)),
            vmem((3, 8, 128)),
            vmem((8, 128)),
            vmem((8, 128)),
            vmem((2, 8, 128)),
            vmem((7, 8, 128)),
            vmem((31, 8, 128)),
            dma((2,)), dma((1,)),
            dma((3,)), dma((3,)), dma((3,)), dma((3,)), dma((4,)), dma((4,)),
            dma((4, 2)), dma((4, 2)), dma((2,)), dma((2,)), dma((3,)), dma((3,)),
            dma((3,)), dma((3,)), dma((7,)), dma((7,)), dma((31,)), dma((31,)),
        ],
        compiler_params=pltpu.CompilerParams(
            collective_id=0, has_side_effects=True, vmem_limit_bytes=48 * 1024 * 1024
        ),
    )(members, conductivity, weights)
    return value * scale[0, 0]


def solution(mesh):
    placed = (P("member", None, "lat", None), P(None, "lat", None), P("member"))
    return jax.shard_map(
        local, mesh=mesh, in_specs=placed, out_specs=P("member", "lat", None), check_vma=False
    )
```

```python
import functools

import jax
import jax.numpy as jnp
from jax import lax
from jax.experimental import pallas as pl
from jax.experimental.pallas import tpu as pltpu
from jax.sharding import PartitionSpec as P

MESH = pl.DeviceIdType.MESH
STEP = 0.16
PASSES = 3
LEV, ROWS, LON = 16, 8, 1440
HALF = LEV // 2
CHUNKS = 4
COLS = LON // CHUNKS
GHOST = 12
TILES = 3
HALO = 3 * PASSES
ALL = ROWS + 2 * HALO
OWN = HALO
INNER = ROWS + 4 * PASSES
LAST = 1408


def lanes():
    return lax.broadcasted_iota(jnp.int32, (8, 128), 1)


def lane_tiles(ref, lev):
    tiles = [ref[lev, :, pl.ds(128 * i, 128)] for i in range(11)]
    return tiles + [jnp.concatenate([ref[lev, :, pl.ds(LAST, LON - LAST)], tiles[0][:, : 128 - (LON - LAST)]], axis=1)]


def chunk_tile(tiles, part, t):
    lane = lanes()
    start = COLS * part - GHOST
    shift = start % 128
    at = shift + 3 * lane + t
    if part == 0:
        window = [tiles[11], tiles[0], tiles[1], tiles[2]]
        index = jnp.where(at < 128, at - 96, at % 128)
        edges = [128, 256, 384]
    else:
        window = [tiles[start // 128 + i] for i in range(4)]
        index = at % 128
        edges = [128, 256, 384]
        if part == CHUNKS - 1:
            window.append(tiles[0])
            wrap = LON - 128 * (start // 128)
            index = jnp.where(at >= wrap, at - wrap, index)
            edges.append(wrap)
    value = jnp.take_along_axis(window[0], index, axis=1)
    for piece, edge in zip(window[1:], edges):
        value = jnp.where(at >= edge, jnp.take_along_axis(piece, index, axis=1), value)
    return value


def joined_tile(chunks, index):
    lane = lanes()
    result = None
    for part in range(CHUNKS):
        low, high = COLS * part, COLS * (part + 1)
        if low >= 128 * (index + 1) or high <= 128 * index:
            continue
        column = 128 * index + lane - low + GHOST
        source = jnp.clip(column // 3, 0, 127)
        kind = column % 3
        pieces = [jnp.take_along_axis(chunks[part][t], source, axis=1) for t in range(TILES)]
        value = jnp.where(kind == 0, pieces[0], jnp.where(kind == 1, pieces[1], pieces[2]))
        result = value if result is None else jnp.where(lane < low - 128 * index, result, value)
    return result


def kernel(
    members, conductivity, weights, out,
    xm, xc, sends, slabs, cond, cond_far, table_s, table_d, table_g, field,
    logs, logs_other, final, final_other, shares, gathered,
    weight_own, weight_in, weight_sum, weight_other, mass, column_in, plane_in,
    load_sem, local_sem, z_send, z_recv, w_send, w_recv, c_send, c_recv, y_send, y_recv, f_send, f_recv,
    s_send, s_recv, g_send, g_recv, t_send, t_recv, p_send, p_recv,
):
    me = lax.axis_index("member")
    lat = lax.axis_index("lat")
    zone, core = me // 2, lax.rem(me, 2)
    lat_count = lax.axis_size("lat")

    def zone_peer(k):
        return {"member": lax.rem(zone + k, CHUNKS) * 2 + core}

    def lat_peer(k):
        return {"lat": lax.rem(lat + k + lat_count, lat_count)}

    sibling = {"member": me + 1 - 2 * core}

    def column_peer(k):
        place = lax.rem(2 * zone + lat // 32 + k, 8)
        return {"member": place // 2 * 2 + core, "lat": lax.rem(place, 2) * 32 + lax.rem(lat, 32)}

    def plane_peer(k):
        return {"lat": lat // 32 * 32 + lax.rem(lat + k, 32)}

    load_m = pltpu.make_async_copy(members.at[0], xm, load_sem.at[1])
    load_c = pltpu.make_async_copy(conductivity, xc, load_sem.at[0])
    load_m.start()
    load_c.start()

    barrier = pltpu.get_barrier_semaphore()
    partners = [lat_peer(k) for k in (1, -1, 2, -2)] + [sibling] + [column_peer(k) for k in range(1, 8)]
    for partner in partners:
        pl.semaphore_signal(barrier, inc=1, device_id=partner, device_id_type=MESH)

    def greet(k, carry):
        pl.semaphore_signal(barrier, inc=1, device_id=plane_peer(k), device_id_type=MESH)
        return carry

    lax.fori_loop(1, 32, greet, 0)

    def remote(src, dst, send, recv, target):
        return pltpu.make_async_remote_copy(
            src_ref=src, dst_ref=dst, send_sem=send, recv_sem=recv, device_id=target, device_id_type=MESH
        )

    load_m.wait()

    def member_chunks(lev, carry):
        half = lev // HALF
        place = jnp.where(half == 0, lev, LEV - 1 - lev)
        tiles = lane_tiles(xm, lev)
        for part in range(CHUNKS):
            for t in range(TILES):
                sends[part, t, place, pl.ds(pl.multiple_of(8 * half, 8), 8), :] = chunk_tile(tiles, part, t)
        return carry

    lax.fori_loop(0, LEV, member_chunks, 0)
    load_c.wait()
    for part in range(CHUNKS):

        @pl.when(zone == part)
        def _(part=part):
            def cond_chunk(lev, carry):
                place = jnp.where(lev < HALF, lev, HALF + LEV - 1 - lev)
                tiles = lane_tiles(xc, lev)
                for t in range(TILES):
                    cond[1, place, t] = chunk_tile(tiles, part, t)
                return carry

            lax.fori_loop(0, LEV, cond_chunk, 0)

    weight_own[...] = jnp.full((8, 128), weights[0], jnp.float32)
    pl.semaphore_wait(barrier, len(partners) + 31)

    def block(b):
        return pl.ds(pl.multiple_of(16 * b, 16), 16)

    zone_copies = {
        (k, t): remote(
            sends.at[lax.rem(zone + k, CHUNKS), t], slabs.at[1, t, :, block(zone), :],
            z_send.at[k - 1, t], z_recv.at[k - 1, t], zone_peer(k),
        )
        for k in (1, 3, 2)
        for t in range(TILES)
    }
    for t in range(TILES):
        for k in (1, 3):
            zone_copies[k, t].start()
    mine = pltpu.make_async_copy(sends.at[zone], slabs.at[1, :, :, block(zone), :], local_sem.at[0])
    mine.start()

    own_half = pl.ds(pl.multiple_of(HALF * core, HALF), HALF)
    far_up = (cond.at[1, own_half, :, pl.ds(7, 1), :], cond_far.at[0, own_half, :, pl.ds(0, 1), :])
    far_down = (cond.at[1, own_half, :, pl.ds(0, 1), :], cond_far.at[1, own_half, :, pl.ds(0, 1), :])
    cond_copies = [
        remote(cond.at[1, own_half], cond.at[0, own_half], c_send.at[0], c_recv.at[0], lat_peer(1)),
        remote(cond.at[1, own_half], cond.at[2, own_half], c_send.at[1], c_recv.at[1], lat_peer(-1)),
        remote(*far_up, c_send.at[2], c_recv.at[2], lat_peer(2)),
        remote(*far_down, c_send.at[3], c_recv.at[3], lat_peer(-2)),
    ]
    for copy in cond_copies:
        copy.start()
    weight_copies = [
        remote(weight_own, weight_in.at[k - 1], w_send.at[k - 1], w_recv.at[k - 1], zone_peer(k)) for k in (1, 2, 3)
    ]
    for copy in weight_copies:
        copy.start()

    def forward(k, t):
        source = lax.rem(zone - k + CHUNKS, CHUNKS)
        part = slabs.at[1, t, :, block(source), :]
        return [
            remote(part, slabs.at[0, t, :, block(source), :], y_send.at[k, t, 0], y_recv.at[k, t, 0], lat_peer(1)),
            remote(part, slabs.at[2, t, :, block(source), :], y_send.at[k, t, 1], y_recv.at[k, t, 1], lat_peer(-1)),
        ]

    row_copies = []

    def pass_on(k, t):
        for copy in forward(k, t):
            copy.start()
            row_copies.append(copy)

    mine.wait()
    for t in range(TILES):
        pass_on(0, t)

    sub = lax.broadcasted_iota(jnp.int32, (8, 128), 0)
    even = sub % 2 == 0

    def spread(low, high):
        return jnp.where(even, jnp.broadcast_to(low, (8, 128)), jnp.broadcast_to(high, (8, 128)))

    def swap_halves(value):
        return jnp.where(even, pltpu.roll(value, 7, 0), pltpu.roll(value, 1, 0))

    def sides(value):
        west, east = pltpu.roll(value[2], 1, 1), pltpu.roll(value[0], 127, 1)
        return [west + value[1], value[0] + value[2], value[1] + east]

    def stencil(src, row, place):
        value = [src[row, place, t] for t in range(TILES)]
        total = sides(value)
        for t in range(TILES):
            total[t] = total[t] + (src[row - 1, place, t] + src[row + 1, place, t])
            if place > 0:
                total[t] = total[t] + src[row, place - 1, t]
            total[t] = total[t] + (src[row, place + 1, t] if place < HALF - 1 else swap_halves(value[t]))
        return value, total

    inside_low = jnp.where(lat == 0, 0.0, 1.0)
    inside_high = jnp.where(lat == lat_count - 1, 0.0, 1.0)
    far_low = jnp.where(lat <= 1, 0.0, 1.0)
    far_high = jnp.where(lat >= lat_count - 2, 0.0, 1.0)

    def root_rows(ref, source, count, first, inside):
        def body(row, carry):
            for place in range(HALF):
                for t in range(TILES):
                    low = ref[source, place, t, pl.ds(row, 1), :]
                    high = ref[source, HALF + place, t, pl.ds(row, 1), :]
                    table_s[first + row, place, t] = jnp.sqrt(spread(low, high)) * inside
            return carry

        lax.fori_loop(0, count, body, 0)

    def table_rows(low, high):
        def body(row, carry):
            for place in range(HALF):
                value, total = stencil(table_s, row, place)
                for t in range(TILES):
                    table_d[row, place, t] = 1.0 - STEP * (value[t] * total[t])
                    table_g[row, place, t] = STEP * (value[t] * value[t])
            return carry

        lax.fori_loop(low, high, body, 0)

    def start_rows(slab, first):
        def body(row, carry):
            for place in range(HALF):
                for t in range(TILES):
                    value = slabs[slab, t, place, pl.ds(row, 8, stride=8), :]
                    field[2, first + row, place, t] = value * table_s[first + row, place, t]
            return carry

        lax.fori_loop(0, ROWS, body, 0)

    root_rows(cond, 1, ROWS, OWN, 1.0)
    for copy in cond_copies:
        copy.wait()
    hand_copies = [
        remote(cond.at[0, own_half], cond.at[0, own_half], c_send.at[4], c_recv.at[4], sibling),
        remote(cond.at[2, own_half], cond.at[2, own_half], c_send.at[5], c_recv.at[5], sibling),
        remote(cond_far.at[:, own_half], cond_far.at[:, own_half], c_send.at[6], c_recv.at[6], sibling),
    ]
    for copy in hand_copies:
        copy.start()
    for k in (1, 3):
        zone_copies[k, 0].wait_recv()
        pass_on(k, 0)
    for t in range(TILES):
        zone_copies[2, t].start()
    for copy in hand_copies:
        copy.wait()
    root_rows(cond, 0, ROWS, OWN - ROWS, inside_low)
    root_rows(cond, 2, ROWS, OWN + ROWS, inside_high)
    root_rows(cond_far, 0, 1, 0, far_low)
    root_rows(cond_far, 1, 1, ALL - 1, far_high)
    for k in (1, 3):
        zone_copies[k, 1].wait_recv()
        pass_on(k, 1)
    table_rows(1, ALL // 2)
    for k in (1, 3):
        zone_copies[k, 2].wait_recv()
        pass_on(k, 2)
    table_rows(ALL // 2, ALL - 1)
    for t in range(TILES):
        zone_copies[2, t].wait_recv()
        pass_on(2, t)
    start_rows(1, OWN)
    far_copies = [
        remote(field.at[2, OWN + ROWS - 1], field.at[2, 0], f_send.at[0], f_recv.at[0], lat_peer(2)),
        remote(field.at[2, OWN], field.at[2, ALL - 1], f_send.at[1], f_recv.at[1], lat_peer(-2)),
    ]
    for copy in far_copies:
        copy.start()
    for copy in weight_copies:
        copy.wait()
    group = sub // 2
    weight = jnp.zeros((8, 128), jnp.float32)
    total_weight = weight_own[...]
    for k in range(CHUNKS):
        value = weight_own[...] if k == 0 else weight_in[k - 1]
        weight = jnp.where(group == lax.rem(zone - k + CHUNKS, CHUNKS), value, weight)
        if k > 0:
            total_weight = total_weight + value
    weight_sum[...] = total_weight

    for copy in row_copies:
        copy.wait_recv()
    start_rows(0, OWN - ROWS)
    start_rows(2, OWN + ROWS)
    for copy in far_copies:
        copy.wait_recv()
    for row, inside in ((0, far_low), (ALL - 1, far_high)):
        for place in range(HALF):
            for t in range(TILES):
                field[2, row, place, t] = field[2, row, place, t] * inside

    def heat(first_source, first_pass):
        def one_pass(i, carry):
            index = first_pass + i
            low = (index - 1) // 2 * 2 + 1
            dst = lax.rem(i, 2)
            src = jnp.where(i == 0, first_source, 1 - dst)
            here = field.at[src]

            def rows(j, inner):
                for place in range(HALF):
                    for r in range(4):
                        row = low + 4 * j + r
                        value, total = stencil(here, row, place)
                        for t in range(TILES):
                            field[dst, row, place, t] = (
                                table_d[row, place, t] * value[t] + table_g[row, place, t] * total[t]
                            )
                return inner

            return lax.fori_loop(0, (ALL - 2 * low) // 4, rows, carry)

        lax.fori_loop(0, PASSES, one_pass, 0)

    def guarded(value):
        return jnp.where(value > 0.0, value, 1.0)

    upper = sub >= 4
    odd_pair = (sub // 2) % 2 == 1

    def fold(a, b, c, d):
        def halves(x, y):
            return jnp.where(upper, y, x) + pltpu.roll(jnp.where(upper, x, y), 4, 0)

        x, y = halves(a, c), halves(b, d)
        other = jnp.where(odd_pair, pltpu.roll(y, 2, 0), pltpu.roll(x, 6, 0))
        return jnp.where(odd_pair, y, x) + other

    def log_sums(row, q, t):
        return fold(*[weight * jnp.log(guarded(field[0, row, 4 * q + j, t])) for j in range(4)])

    heat(2, 1)

    def first_logs(i, carry):
        for q in range(2):
            for t in range(TILES):
                logs[i, q, t] = log_sums(i + PASSES, q, t)
        return carry

    mid = INNER // 2
    sibling_copies = [
        remote(weight_sum, weight_other, s_send.at[0], s_recv.at[0], sibling),
        remote(logs.at[pl.ds(0, mid)], logs_other.at[pl.ds(0, mid)], s_send.at[1], s_recv.at[1], sibling),
        remote(logs.at[pl.ds(mid, mid)], logs_other.at[pl.ds(mid, mid)], s_send.at[2], s_recv.at[2], sibling),
    ]
    sibling_copies[0].start()
    lax.fori_loop(0, mid, first_logs, 0)
    sibling_copies[1].start()
    lax.fori_loop(mid, INNER, first_logs, 0)
    sibling_copies[2].start()
    sibling_copies[0].wait()
    inverse = 1.0 / (weight_sum[...] + weight_other[...])

    def rescale(i, carry):
        row = i + PASSES
        for q in range(2):
            for t in range(TILES):
                logs_other[i, q, t] = jnp.exp((logs[i, q, t] + logs_other[i, q, t]) * inverse)
        for place in range(HALF):
            q, j = place // 4, place % 4
            for t in range(TILES):
                power = spread(logs_other[i, q, t, pl.ds(2 * j, 1), :], logs_other[i, q, t, pl.ds(2 * j + 1, 1), :])
                field[1, row, place, t] = table_s[row, place, t] * power / guarded(field[0, row, place, t])
        return carry

    sibling_copies[1].wait()
    lax.fori_loop(0, mid, rescale, 0)
    sibling_copies[2].wait()
    lax.fori_loop(mid, INNER, rescale, 0)
    heat(1, 1 + PASSES)

    def ratio(row, carry):
        for place in range(HALF):
            for t in range(TILES):
                top = field[2, row, place, t] * table_s[row, place, t]
                field[1, row, place, t] = top / guarded(field[0, row, place, t])
        return carry

    lax.fori_loop(2 * PASSES, ALL - 2 * PASSES, ratio, 0)
    heat(1, 1 + 2 * PASSES)

    def second_logs(i, carry):
        for q in range(2):
            for t in range(TILES):
                final[t, q, pl.ds(pl.multiple_of(8 * i, 8), 8), :] = log_sums(i + OWN, q, t)
        return carry

    lax.fori_loop(0, ROWS, second_logs, 0)
    final_copy = remote(final, final_other, s_send.at[3], s_recv.at[3], sibling)
    final_copy.start()
    final_copy.wait()
    valid = []
    for t in range(TILES):
        at = 3 * lanes() + t
        valid.append((at >= GHOST) & (at < GHOST + COLS))
    summed = jnp.zeros((8, 128), jnp.float32)
    for lev in range(LEV):
        half, place = (0, lev) if lev < HALF else (1, LEV - 1 - lev)
        across = pl.ds(2 * (place % 4) + half, 8, stride=8)
        for t in range(TILES):
            value = jnp.exp((final[t, place // 4, across, :] + final_other[t, place // 4, across, :]) * inverse)
            value = value * lax.rsqrt(cond[1, HALF * half + place, t])
            summed = summed + jnp.where(valid[t], value, 0.0)
            shares[lev // 4, lev // 2 % 2, lev % 2, t] = value

    mass[0] = summed
    column_copies = [
        remote(mass.at[0], column_in.at[k - 1], t_send.at[k - 1], t_recv.at[k - 1], column_peer(k)) for k in range(1, 8)
    ]
    for copy in column_copies:
        copy.start()
    share_copies = [
        remote(
            shares.at[lax.rem(zone + k, CHUNKS), core], gathered.at[zone], g_send.at[k - 1], g_recv.at[k - 1],
            zone_peer(k),
        )
        for k in (1, 2, 3)
    ]
    for copy in share_copies:
        copy.start()
    gathered[zone] = shares[zone, core]
    for k, copy in enumerate(column_copies):
        copy.wait()
        summed = summed + column_in[k]

    mass[1] = summed

    def plane_copy(k):
        return remote(mass.at[1], plane_in.at[k - 1], p_send.at[k - 1], p_recv.at[k - 1], plane_peer(k))

    def send_plane(k, carry):
        plane_copy(k).start()
        return carry

    lax.fori_loop(1, 32, send_plane, 0)
    for copy in share_copies:
        copy.wait()
    joined = []
    for i in range(2):
        chunks = [[gathered[part, i, t] for t in range(TILES)] for part in range(CHUNKS)]
        joined.append([joined_tile(chunks, index) for index in range(12)])
    for t in range(TILES):
        for k in (1, 2, 3):
            zone_copies[k, t].wait_send()
    for copy in row_copies + far_copies:
        copy.wait_send()

    def take_plane(k, value):
        plane_copy(k).wait()
        return value + plane_in[k - 1]

    summed = lax.fori_loop(1, 32, take_plane, summed)
    cells = LEV * ROWS * lat_count * LON
    scale = cells / jnp.sum(summed)
    for i in range(2):
        for index in range(11):
            out[i, :, pl.ds(128 * index, 128)] = joined[i][index] * scale
        out[i, :, pl.ds(LAST, LON - LAST)] = (joined[i][11] * scale)[:, : LON - LAST]


def local(members, conductivity, weights):
    vmem = functools.partial(pltpu.VMEM, dtype=jnp.float32)
    dma = pltpu.SemaphoreType.DMA
    tiled = (TILES, 8, 128)
    table = (ALL, HALF) + tiled
    return pl.pallas_call(
        kernel,
        name="barycenter",
        out_shape=jax.ShapeDtypeStruct((2, ROWS, LON), jnp.float32),
        in_specs=[
            pl.BlockSpec(memory_space=pl.ANY),
            pl.BlockSpec(memory_space=pl.ANY),
            pl.BlockSpec(memory_space=pltpu.SMEM),
        ],
        out_specs=pl.BlockSpec(memory_space=pltpu.VMEM),
        scratch_shapes=[
            vmem((LEV, ROWS, LON)),
            vmem((LEV, ROWS, LON)),
            vmem((CHUNKS, TILES, HALF, 16, 128)),
            vmem((3, TILES, HALF, 64, 128)),
            vmem((3, LEV) + tiled),
            vmem((2, LEV) + tiled),
            vmem(table), vmem(table), vmem(table),
            vmem((3,) + table),
            vmem((INNER, 2) + tiled),
            vmem((INNER, 2) + tiled),
            vmem((TILES, 2, 64, 128)),
            vmem((TILES, 2, 64, 128)),
            vmem((CHUNKS, 2, 2) + tiled),
            vmem((CHUNKS, 2) + tiled),
            vmem((8, 128)),
            vmem((3, 8, 128)),
            vmem((8, 128)),
            vmem((8, 128)),
            vmem((2, 8, 128)),
            vmem((7, 8, 128)),
            vmem((31, 8, 128)),
            dma((2,)), dma((1,)),
            dma((3, 3)), dma((3, 3)), dma((3,)), dma((3,)), dma((7,)), dma((7,)),
            dma((4, 3, 2)), dma((4, 3, 2)), dma((2,)), dma((2,)), dma((4,)), dma((4,)),
            dma((3,)), dma((3,)), dma((7,)), dma((7,)), dma((31,)), dma((31,)),
        ],
        compiler_params=pltpu.CompilerParams(
            collective_id=0, has_side_effects=True, vmem_limit_bytes=60 * 1024 * 1024
        ),
    )(members, conductivity, weights)


def solution(mesh):
    placed = (P("member", None, "lat", None), P(None, "lat", None), P("member"))
    return jax.shard_map(
        local, mesh=mesh, in_specs=placed, out_specs=P("member", "lat", None), check_vma=False
    )
```

```python
import functools

import jax
import jax.numpy as jnp
from jax import lax
from jax.experimental import pallas as pl
from jax.experimental.pallas import tpu as pltpu
from jax.sharding import PartitionSpec as P

MESH = pl.DeviceIdType.MESH
STEP = 0.16
PASSES = 3
LEV, ROWS, LON = 16, 8, 1440
HALF = LEV // 2
CHUNKS = 4
COLS = LON // CHUNKS
GHOST = 12
TILES = 3
HALO = 3 * PASSES
ALL = ROWS + 2 * HALO
OWN = HALO
INNER = ROWS + 4 * PASSES
LAST = 1408


def lanes():
    return lax.broadcasted_iota(jnp.int32, (8, 128), 1)


def lane_tiles(ref, lev):
    tiles = [ref[lev, :, pl.ds(128 * i, 128)] for i in range(11)]
    return tiles + [jnp.concatenate([ref[lev, :, pl.ds(LAST, LON - LAST)], tiles[0][:, : 128 - (LON - LAST)]], axis=1)]


def chunk_tile(tiles, part, t):
    lane = lanes()
    start = COLS * part - GHOST
    shift = start % 128
    at = shift + 3 * lane + t
    if part == 0:
        window = [tiles[11], tiles[0], tiles[1], tiles[2]]
        index = jnp.where(at < 128, at - 96, at % 128)
        edges = [128, 256, 384]
    else:
        window = [tiles[start // 128 + i] for i in range(4)]
        index = at % 128
        edges = [128, 256, 384]
        if part == CHUNKS - 1:
            window.append(tiles[0])
            wrap = LON - 128 * (start // 128)
            index = jnp.where(at >= wrap, at - wrap, index)
            edges.append(wrap)
    value = jnp.take_along_axis(window[0], index, axis=1)
    for piece, edge in zip(window[1:], edges):
        value = jnp.where(at >= edge, jnp.take_along_axis(piece, index, axis=1), value)
    return value


def joined_tile(chunks, index):
    lane = lanes()
    result = None
    for part in range(CHUNKS):
        low, high = COLS * part, COLS * (part + 1)
        if low >= 128 * (index + 1) or high <= 128 * index:
            continue
        column = 128 * index + lane - low + GHOST
        source = jnp.clip(column // 3, 0, 127)
        kind = column % 3
        pieces = [jnp.take_along_axis(chunks[part][t], source, axis=1) for t in range(TILES)]
        value = jnp.where(kind == 0, pieces[0], jnp.where(kind == 1, pieces[1], pieces[2]))
        result = value if result is None else jnp.where(lane < low - 128 * index, result, value)
    return result


def kernel(
    members, conductivity, weights, out,
    xm, xc, sends, slabs, cond, cond_far, table_s, table_d, table_g, start, buf_a, buf_b,
    logs, logs_other, final, final_other, shares, gathered,
    weight_own, weight_in, weight_sum, weight_other, mass, column_in, plane_in,
    load_sem, local_sem, z_send, z_recv, w_send, w_recv, c_send, c_recv, y_send, y_recv, f_send, f_recv,
    s_send, s_recv, g_send, g_recv, t_send, t_recv, p_send, p_recv,
):
    me = lax.axis_index("member")
    lat = lax.axis_index("lat")
    zone, core = me // 2, lax.rem(me, 2)
    lat_count = lax.axis_size("lat")

    def zone_peer(k):
        return {"member": lax.rem(zone + k, CHUNKS) * 2 + core}

    def lat_peer(k):
        return {"lat": lax.rem(lat + k + lat_count, lat_count)}

    sibling = {"member": me + 1 - 2 * core}

    def column_peer(k):
        place = lax.rem(2 * zone + lat // 32 + k, 8)
        return {"member": place // 2 * 2 + core, "lat": lax.rem(place, 2) * 32 + lax.rem(lat, 32)}

    def plane_peer(k):
        return {"lat": lat // 32 * 32 + lax.rem(lat + k, 32)}

    load_m = pltpu.make_async_copy(members.at[0], xm, load_sem.at[1])
    load_c = pltpu.make_async_copy(conductivity, xc, load_sem.at[0])
    load_m.start()
    load_c.start()

    barrier = pltpu.get_barrier_semaphore()
    partners = [lat_peer(k) for k in (1, -1, 2, -2)] + [sibling] + [column_peer(k) for k in range(1, 8)]
    for partner in partners:
        pl.semaphore_signal(barrier, inc=1, device_id=partner, device_id_type=MESH)

    def greet(k, carry):
        pl.semaphore_signal(barrier, inc=1, device_id=plane_peer(k), device_id_type=MESH)
        return carry

    lax.fori_loop(1, 32, greet, 0)

    def remote(src, dst, send, recv, target):
        return pltpu.make_async_remote_copy(
            src_ref=src, dst_ref=dst, send_sem=send, recv_sem=recv, device_id=target, device_id_type=MESH
        )

    load_m.wait()

    def member_chunks(lev, carry):
        half = lev // HALF
        place = jnp.where(half == 0, lev, LEV - 1 - lev)
        tiles = lane_tiles(xm, lev)
        for part in range(CHUNKS):
            for t in range(TILES):
                sends[part, t, place, pl.ds(pl.multiple_of(8 * half, 8), 8), :] = chunk_tile(tiles, part, t)
        return carry

    lax.fori_loop(0, LEV, member_chunks, 0)
    load_c.wait()
    for part in range(CHUNKS):

        @pl.when(zone == part)
        def _(part=part):
            def cond_chunk(lev, carry):
                place = jnp.where(lev < HALF, lev, HALF + LEV - 1 - lev)
                tiles = lane_tiles(xc, lev)
                for t in range(TILES):
                    cond[1, place, t] = chunk_tile(tiles, part, t)
                return carry

            lax.fori_loop(0, LEV, cond_chunk, 0)

    weight_own[...] = jnp.full((8, 128), weights[0], jnp.float32)
    pl.semaphore_wait(barrier, len(partners) + 31)

    def block(b):
        return pl.ds(pl.multiple_of(16 * b, 16), 16)

    zone_copies = {
        (k, t): remote(
            sends.at[lax.rem(zone + k, CHUNKS), t], slabs.at[1, t, :, block(zone), :],
            z_send.at[k - 1, t], z_recv.at[k - 1, t], zone_peer(k),
        )
        for k in (1, 3, 2)
        for t in range(TILES)
    }
    for t in range(TILES):
        for k in (1, 3):
            zone_copies[k, t].start()
    mine = pltpu.make_async_copy(sends.at[zone], slabs.at[1, :, :, block(zone), :], local_sem.at[0])
    mine.start()

    own_half = pl.ds(pl.multiple_of(HALF * core, HALF), HALF)
    far_up = (cond.at[1, own_half, :, pl.ds(7, 1), :], cond_far.at[0, own_half, :, pl.ds(0, 1), :])
    far_down = (cond.at[1, own_half, :, pl.ds(0, 1), :], cond_far.at[1, own_half, :, pl.ds(0, 1), :])
    cond_copies = [
        remote(cond.at[1, own_half], cond.at[0, own_half], c_send.at[0], c_recv.at[0], lat_peer(1)),
        remote(cond.at[1, own_half], cond.at[2, own_half], c_send.at[1], c_recv.at[1], lat_peer(-1)),
        remote(*far_up, c_send.at[2], c_recv.at[2], lat_peer(2)),
        remote(*far_down, c_send.at[3], c_recv.at[3], lat_peer(-2)),
    ]
    for copy in cond_copies:
        copy.start()
    weight_copies = [
        remote(weight_own, weight_in.at[k - 1], w_send.at[k - 1], w_recv.at[k - 1], zone_peer(k)) for k in (1, 2, 3)
    ]
    for copy in weight_copies:
        copy.start()

    def forward(k, t):
        source = lax.rem(zone - k + CHUNKS, CHUNKS)
        part = slabs.at[1, t, :, block(source), :]
        return [
            remote(part, slabs.at[0, t, :, block(source), :], y_send.at[k, t, 0], y_recv.at[k, t, 0], lat_peer(1)),
            remote(part, slabs.at[2, t, :, block(source), :], y_send.at[k, t, 1], y_recv.at[k, t, 1], lat_peer(-1)),
        ]

    row_copies = []

    def pass_on(k, t):
        for copy in forward(k, t):
            copy.start()
            row_copies.append(copy)

    mine.wait()
    for t in range(TILES):
        pass_on(0, t)

    sub = lax.broadcasted_iota(jnp.int32, (8, 128), 0)
    even = sub % 2 == 0

    def spread(low, high):
        return jnp.where(even, jnp.broadcast_to(low, (8, 128)), jnp.broadcast_to(high, (8, 128)))

    def swap_halves(value):
        return jnp.where(even, pltpu.roll(value, 7, 0), pltpu.roll(value, 1, 0))

    def sides(value):
        west, east = pltpu.roll(value[2], 1, 1), pltpu.roll(value[0], 127, 1)
        return [west + value[1], value[0] + value[2], value[1] + east]

    def stencil(src, row, place):
        value = [src[row, place, t] for t in range(TILES)]
        total = sides(value)
        for t in range(TILES):
            total[t] = total[t] + (src[row - 1, place, t] + src[row + 1, place, t])
            if place > 0:
                total[t] = total[t] + src[row, place - 1, t]
            total[t] = total[t] + (src[row, place + 1, t] if place < HALF - 1 else swap_halves(value[t]))
        return value, total

    inside_low = jnp.where(lat == 0, 0.0, 1.0)
    inside_high = jnp.where(lat == lat_count - 1, 0.0, 1.0)
    far_low = jnp.where(lat <= 1, 0.0, 1.0)
    far_high = jnp.where(lat >= lat_count - 2, 0.0, 1.0)

    def root_rows(ref, source, count, first, inside):
        def body(row, carry):
            for place in range(HALF):
                for t in range(TILES):
                    low = ref[source, place, t, pl.ds(row, 1), :]
                    high = ref[source, HALF + place, t, pl.ds(row, 1), :]
                    table_s[first + row, place, t] = jnp.sqrt(spread(low, high)) * inside
            return carry

        lax.fori_loop(0, count, body, 0)

    def table_rows(low, high):
        def body(row, carry):
            for place in range(HALF):
                value, total = stencil(table_s, row, place)
                for t in range(TILES):
                    table_d[row, place, t] = 1.0 - STEP * (value[t] * total[t])
                    table_g[row, place, t] = STEP * (value[t] * value[t])
            return carry

        lax.fori_loop(low, high, body, 0)

    def start_rows(slab, first):
        def body(row, carry):
            for place in range(HALF):
                for t in range(TILES):
                    value = slabs[slab, t, place, pl.ds(row, 8, stride=8), :]
                    start[first + row, place, t] = value * table_s[first + row, place, t]
            return carry

        lax.fori_loop(0, ROWS, body, 0)

    root_rows(cond, 1, ROWS, OWN, 1.0)
    for copy in cond_copies:
        copy.wait()
    hand_copies = [
        remote(cond.at[0, own_half], cond.at[0, own_half], c_send.at[4], c_recv.at[4], sibling),
        remote(cond.at[2, own_half], cond.at[2, own_half], c_send.at[5], c_recv.at[5], sibling),
        remote(cond_far.at[:, own_half], cond_far.at[:, own_half], c_send.at[6], c_recv.at[6], sibling),
    ]
    for copy in hand_copies:
        copy.start()
    for k in (1, 3):
        zone_copies[k, 0].wait_recv()
        pass_on(k, 0)
    for t in range(TILES):
        zone_copies[2, t].start()
    for copy in hand_copies:
        copy.wait()
    root_rows(cond, 0, ROWS, OWN - ROWS, inside_low)
    root_rows(cond, 2, ROWS, OWN + ROWS, inside_high)
    root_rows(cond_far, 0, 1, 0, far_low)
    root_rows(cond_far, 1, 1, ALL - 1, far_high)
    for k in (1, 3):
        zone_copies[k, 1].wait_recv()
        pass_on(k, 1)
    table_rows(1, ALL // 2)
    for k in (1, 3):
        zone_copies[k, 2].wait_recv()
        pass_on(k, 2)
    table_rows(ALL // 2, ALL - 1)
    for t in range(TILES):
        zone_copies[2, t].wait_recv()
        pass_on(2, t)
    start_rows(1, OWN)
    far_copies = [
        remote(start.at[OWN + ROWS - 1], start.at[0], f_send.at[0], f_recv.at[0], lat_peer(2)),
        remote(start.at[OWN], start.at[ALL - 1], f_send.at[1], f_recv.at[1], lat_peer(-2)),
    ]
    for copy in far_copies:
        copy.start()
    for copy in weight_copies:
        copy.wait()
    group = sub // 2
    weight = jnp.zeros((8, 128), jnp.float32)
    total_weight = weight_own[...]
    for k in range(CHUNKS):
        value = weight_own[...] if k == 0 else weight_in[k - 1]
        weight = jnp.where(group == lax.rem(zone - k + CHUNKS, CHUNKS), value, weight)
        if k > 0:
            total_weight = total_weight + value
    weight_sum[...] = total_weight

    for copy in row_copies:
        copy.wait_recv()
    start_rows(0, OWN - ROWS)
    start_rows(2, OWN + ROWS)
    for copy in far_copies:
        copy.wait_recv()
    for row, inside in ((0, far_low), (ALL - 1, far_high)):
        for place in range(HALF):
            for t in range(TILES):
                start[row, place, t] = start[row, place, t] * inside

    def heat(src, dst, index):
        low = (index - 1) // 2 * 2 + 1

        def rows(j, carry):
            for place in range(HALF):
                for r in range(4):
                    row = low + 4 * j + r
                    value, total = stencil(src, row, place)
                    for t in range(TILES):
                        dst[row, place, t] = table_d[row, place, t] * value[t] + table_g[row, place, t] * total[t]
            return carry

        lax.fori_loop(0, (ALL - 2 * low) // 4, rows, 0)

    def guarded(value):
        return jnp.where(value > 0.0, value, 1.0)

    upper = sub >= 4
    odd_pair = (sub // 2) % 2 == 1

    def fold(a, b, c, d):
        def halves(x, y):
            return jnp.where(upper, y, x) + pltpu.roll(jnp.where(upper, x, y), 4, 0)

        x, y = halves(a, c), halves(b, d)
        other = jnp.where(odd_pair, pltpu.roll(y, 2, 0), pltpu.roll(x, 6, 0))
        return jnp.where(odd_pair, y, x) + other

    def log_sums(row, q, t):
        return fold(*[weight * jnp.log(guarded(buf_a[row, 4 * q + j, t])) for j in range(4)])

    heat(start, buf_a, 1)
    heat(buf_a, buf_b, 2)
    heat(buf_b, buf_a, 3)

    def first_logs(i, carry):
        for q in range(2):
            for t in range(TILES):
                logs[i, q, t] = log_sums(i + PASSES, q, t)
        return carry

    mid = INNER // 2
    sibling_copies = [
        remote(weight_sum, weight_other, s_send.at[0], s_recv.at[0], sibling),
        remote(logs.at[pl.ds(0, mid)], logs_other.at[pl.ds(0, mid)], s_send.at[1], s_recv.at[1], sibling),
        remote(logs.at[pl.ds(mid, mid)], logs_other.at[pl.ds(mid, mid)], s_send.at[2], s_recv.at[2], sibling),
    ]
    sibling_copies[0].start()
    lax.fori_loop(0, mid, first_logs, 0)
    sibling_copies[1].start()
    lax.fori_loop(mid, INNER, first_logs, 0)
    sibling_copies[2].start()
    sibling_copies[0].wait()
    inverse = 1.0 / (weight_sum[...] + weight_other[...])

    def rescale(i, carry):
        row = i + PASSES
        for q in range(2):
            for t in range(TILES):
                logs_other[i, q, t] = jnp.exp((logs[i, q, t] + logs_other[i, q, t]) * inverse)
        for place in range(HALF):
            q, j = place // 4, place % 4
            for t in range(TILES):
                power = spread(logs_other[i, q, t, pl.ds(2 * j, 1), :], logs_other[i, q, t, pl.ds(2 * j + 1, 1), :])
                buf_b[row, place, t] = table_s[row, place, t] * power / guarded(buf_a[row, place, t])
        return carry

    sibling_copies[1].wait()
    lax.fori_loop(0, mid, rescale, 0)
    sibling_copies[2].wait()
    lax.fori_loop(mid, INNER, rescale, 0)
    heat(buf_b, buf_a, 4)
    heat(buf_a, buf_b, 5)
    heat(buf_b, buf_a, 6)

    def ratio(row, carry):
        for place in range(HALF):
            for t in range(TILES):
                top = start[row, place, t] * table_s[row, place, t]
                buf_b[row, place, t] = top / guarded(buf_a[row, place, t])
        return carry

    lax.fori_loop(2 * PASSES, ALL - 2 * PASSES, ratio, 0)
    heat(buf_b, buf_a, 7)
    heat(buf_a, buf_b, 8)
    heat(buf_b, buf_a, 9)

    def second_logs(i, carry):
        for q in range(2):
            for t in range(TILES):
                final[t, q, pl.ds(pl.multiple_of(8 * i, 8), 8), :] = log_sums(i + OWN, q, t)
        return carry

    lax.fori_loop(0, ROWS, second_logs, 0)
    final_copy = remote(final, final_other, s_send.at[3], s_recv.at[3], sibling)
    final_copy.start()
    final_copy.wait()
    valid = []
    for t in range(TILES):
        at = 3 * lanes() + t
        valid.append((at >= GHOST) & (at < GHOST + COLS))
    summed = jnp.zeros((8, 128), jnp.float32)
    for lev in range(LEV):
        half, place = (0, lev) if lev < HALF else (1, LEV - 1 - lev)
        across = pl.ds(2 * (place % 4) + half, 8, stride=8)
        for t in range(TILES):
            value = jnp.exp((final[t, place // 4, across, :] + final_other[t, place // 4, across, :]) * inverse)
            value = value * lax.rsqrt(cond[1, HALF * half + place, t])
            summed = summed + jnp.where(valid[t], value, 0.0)
            shares[lev // 4, lev // 2 % 2, lev % 2, t] = value

    mass[0] = summed
    column_copies = [
        remote(mass.at[0], column_in.at[k - 1], t_send.at[k - 1], t_recv.at[k - 1], column_peer(k)) for k in range(1, 8)
    ]
    for copy in column_copies:
        copy.start()
    share_copies = [
        remote(
            shares.at[lax.rem(zone + k, CHUNKS), core], gathered.at[zone], g_send.at[k - 1], g_recv.at[k - 1],
            zone_peer(k),
        )
        for k in (1, 2, 3)
    ]
    for copy in share_copies:
        copy.start()
    gathered[zone] = shares[zone, core]
    for k, copy in enumerate(column_copies):
        copy.wait()
        summed = summed + column_in[k]

    mass[1] = summed

    def plane_copy(k):
        return remote(mass.at[1], plane_in.at[k - 1], p_send.at[k - 1], p_recv.at[k - 1], plane_peer(k))

    def send_plane(k, carry):
        plane_copy(k).start()
        return carry

    lax.fori_loop(1, 32, send_plane, 0)
    for copy in share_copies:
        copy.wait()
    joined = []
    for i in range(2):
        chunks = [[gathered[part, i, t] for t in range(TILES)] for part in range(CHUNKS)]
        joined.append([joined_tile(chunks, index) for index in range(12)])
    for t in range(TILES):
        for k in (1, 2, 3):
            zone_copies[k, t].wait_send()
    for copy in row_copies + far_copies:
        copy.wait_send()

    def take_plane(k, value):
        plane_copy(k).wait()
        return value + plane_in[k - 1]

    summed = lax.fori_loop(1, 32, take_plane, summed)
    cells = LEV * ROWS * lat_count * LON
    scale = cells / jnp.sum(summed)
    for i in range(2):
        for index in range(11):
            out[i, :, pl.ds(128 * index, 128)] = joined[i][index] * scale
        out[i, :, pl.ds(LAST, LON - LAST)] = (joined[i][11] * scale)[:, : LON - LAST]


def local(members, conductivity, weights):
    vmem = functools.partial(pltpu.VMEM, dtype=jnp.float32)
    dma = pltpu.SemaphoreType.DMA
    tiled = (TILES, 8, 128)
    table = (ALL, HALF) + tiled
    return pl.pallas_call(
        kernel,
        name="barycenter",
        out_shape=jax.ShapeDtypeStruct((2, ROWS, LON), jnp.float32),
        in_specs=[
            pl.BlockSpec(memory_space=pl.ANY),
            pl.BlockSpec(memory_space=pl.ANY),
            pl.BlockSpec(memory_space=pltpu.SMEM),
        ],
        out_specs=pl.BlockSpec(memory_space=pltpu.VMEM),
        scratch_shapes=[
            vmem((LEV, ROWS, LON)),
            vmem((LEV, ROWS, LON)),
            vmem((CHUNKS, TILES, HALF, 16, 128)),
            vmem((3, TILES, HALF, 64, 128)),
            vmem((3, LEV) + tiled),
            vmem((2, LEV) + tiled),
            vmem(table), vmem(table), vmem(table),
            vmem(table), vmem(table), vmem(table),
            vmem((INNER, 2) + tiled),
            vmem((INNER, 2) + tiled),
            vmem((TILES, 2, 64, 128)),
            vmem((TILES, 2, 64, 128)),
            vmem((CHUNKS, 2, 2) + tiled),
            vmem((CHUNKS, 2) + tiled),
            vmem((8, 128)),
            vmem((3, 8, 128)),
            vmem((8, 128)),
            vmem((8, 128)),
            vmem((2, 8, 128)),
            vmem((7, 8, 128)),
            vmem((31, 8, 128)),
            dma((2,)), dma((1,)),
            dma((3, 3)), dma((3, 3)), dma((3,)), dma((3,)), dma((7,)), dma((7,)),
            dma((4, 3, 2)), dma((4, 3, 2)), dma((2,)), dma((2,)), dma((4,)), dma((4,)),
            dma((3,)), dma((3,)), dma((7,)), dma((7,)), dma((31,)), dma((31,)),
        ],
        compiler_params=pltpu.CompilerParams(
            collective_id=0, has_side_effects=True, vmem_limit_bytes=60 * 1024 * 1024
        ),
    )(members, conductivity, weights)


def solution(mesh):
    placed = (P("member", None, "lat", None), P(None, "lat", None), P("member"))
    return jax.shard_map(
        local, mesh=mesh, in_specs=placed, out_specs=P("member", "lat", None), check_vma=False
    )
```

```python
import functools

import jax
import jax.numpy as jnp
from jax import lax
from jax.experimental import pallas as pl
from jax.experimental.pallas import tpu as pltpu
from jax.sharding import PartitionSpec as P

MESH = pl.DeviceIdType.MESH
STEP = 0.16
PASSES = 3
LEV, ROWS, LON = 16, 8, 1440
HALF = LEV // 2
CHUNKS = 4
COLS = LON // CHUNKS
GHOST = 12
TILES = 3
HALO = 3 * PASSES
ALL = ROWS + 2 * HALO
OWN = HALO
INNER = ROWS + 4 * PASSES
LAST = 1408


def lanes():
    return lax.broadcasted_iota(jnp.int32, (8, 128), 1)


def lane_tiles(ref, lev):
    tiles = [ref[lev, :, pl.ds(128 * i, 128)] for i in range(11)]
    return tiles + [jnp.concatenate([ref[lev, :, pl.ds(LAST, LON - LAST)], tiles[0][:, : 128 - (LON - LAST)]], axis=1)]


def chunk_tile(tiles, part, t):
    lane = lanes()
    start = COLS * part - GHOST
    shift = start % 128
    at = shift + 3 * lane + t
    if part == 0:
        window = [tiles[11], tiles[0], tiles[1], tiles[2]]
        index = jnp.where(at < 128, at - 96, at % 128)
        edges = [128, 256, 384]
    else:
        window = [tiles[start // 128 + i] for i in range(4)]
        index = at % 128
        edges = [128, 256, 384]
        if part == CHUNKS - 1:
            window.append(tiles[0])
            wrap = LON - 128 * (start // 128)
            index = jnp.where(at >= wrap, at - wrap, index)
            edges.append(wrap)
    value = jnp.take_along_axis(window[0], index, axis=1)
    for piece, edge in zip(window[1:], edges):
        value = jnp.where(at >= edge, jnp.take_along_axis(piece, index, axis=1), value)
    return value


def joined_tile(chunks, index):
    lane = lanes()
    result = None
    for part in range(CHUNKS):
        low, high = COLS * part, COLS * (part + 1)
        if low >= 128 * (index + 1) or high <= 128 * index:
            continue
        column = 128 * index + lane - low + GHOST
        source = jnp.clip(column // 3, 0, 127)
        kind = column % 3
        pieces = [jnp.take_along_axis(chunks[part][t], source, axis=1) for t in range(TILES)]
        value = jnp.where(kind == 0, pieces[0], jnp.where(kind == 1, pieces[1], pieces[2]))
        result = value if result is None else jnp.where(lane < low - 128 * index, result, value)
    return result


def kernel(
    members, conductivity, weights, out,
    xm, xc, sends, slabs, relay, far, cond, cond_far, table_s, table_d, table_g, start, buf_a, buf_b,
    logs, logs_other, final, final_other, shares, gathered,
    weight_own, weight_in, weight_sum, weight_other, mass, column_in, plane_in,
    load_sem, local_sem, r_recv, z_send, z_recv, w_send, w_recv, c_send, c_recv, y_send, y_recv, f_send, f_recv,
    s_send, s_recv, g_send, g_recv, t_send, t_recv, p_send, p_recv,
):
    me = lax.axis_index("member")
    lat = lax.axis_index("lat")
    zone, core = me // 2, lax.rem(me, 2)
    lat_count = lax.axis_size("lat")

    def zone_peer(k):
        return {"member": lax.rem(zone + k, CHUNKS) * 2 + core}

    def lat_peer(k):
        return {"lat": lax.rem(lat + k + lat_count, lat_count)}

    sibling = {"member": me + 1 - 2 * core}

    def column_peer(k):
        place = lax.rem(2 * zone + lat // 32 + k, 8)
        return {"member": place // 2 * 2 + core, "lat": lax.rem(place, 2) * 32 + lax.rem(lat, 32)}

    def plane_peer(k):
        return {"lat": lat // 32 * 32 + lax.rem(lat + k, 32)}

    load_m = pltpu.make_async_copy(members.at[0], xm, load_sem.at[1])
    load_c = pltpu.make_async_copy(conductivity, xc, load_sem.at[0])
    load_m.start()
    load_c.start()

    barrier = pltpu.get_barrier_semaphore()
    partners = [lat_peer(k) for k in (1, -1, 2, -2)] + [sibling] + [column_peer(k) for k in range(1, 8)]
    for partner in partners:
        pl.semaphore_signal(barrier, inc=1, device_id=partner, device_id_type=MESH)

    def greet(k, carry):
        pl.semaphore_signal(barrier, inc=1, device_id=plane_peer(k), device_id_type=MESH)
        return carry

    lax.fori_loop(1, 32, greet, 0)

    def remote(src, dst, send, recv, target):
        return pltpu.make_async_remote_copy(
            src_ref=src, dst_ref=dst, send_sem=send, recv_sem=recv, device_id=target, device_id_type=MESH
        )

    def block(b):
        return pl.ds(pl.multiple_of(16 * b, 16), 16)

    zone_copies = {
        (k, t): remote(
            sends.at[lax.rem(zone + k, CHUNKS), t], slabs.at[1, t, :, block(zone), :],
            z_send.at[k - 1, t], z_recv.at[k - 1, t], zone_peer(k),
        )
        for k in (1, 3, 2)
        for t in range(TILES)
    }
    local_copies = [
        pltpu.make_async_copy(sends.at[zone, t], slabs.at[1, t, :, block(zone), :], local_sem.at[t])
        for t in range(TILES)
    ]
    far_copies = []
    edge_low, edge_high = lat == 0, lat == lat_count - 1
    middle = lat_count // 2
    relayed = {(0, 0): 0, (1, 0): 1, (3, 0): 2, (2, 0): 3, (1, 1): 4, (3, 2): 5}
    step_up = (0, 1, middle - 1, edge_high, lat_count - 1, middle)
    step_down = (1, -1, middle, edge_low, 0, middle - 1)

    def row_copy(k, t, direction):
        side, step = direction[0], direction[1]
        source = lax.rem(zone - k + CHUNKS, CHUNKS)
        part = sends.at[zone, t] if k == 0 else slabs.at[1, t, :, block(source), :]
        return remote(
            part, slabs.at[2 * side, t, :, block(source), :], y_send.at[k, t, side], y_recv.at[k, t, side], lat_peer(step)
        )

    def pass_on(k, t):
        source = lax.rem(zone - k + CHUNKS, CHUNKS)
        part = sends.at[zone, t] if k == 0 else slabs.at[1, t, :, block(source), :]
        for direction in (step_up, step_down):
            side, step, origin, edge, via, target = direction
            if (k, t) in relayed:
                index = relayed[k, t]

                @pl.when((lat != origin) & jnp.logical_not(edge))
                def _():
                    row_copy(k, t, direction).start()

                @pl.when(lat == origin)
                def _():
                    remote(part, relay.at[index], y_send.at[k, t, side], r_recv.at[index], {"lat": via}).start()

            else:

                @pl.when(jnp.logical_not(edge))
                def _():
                    row_copy(k, t, direction).start()

    def relay_on(k, t):
        index = relayed[k, t]
        source = lax.rem(zone - k + CHUNKS, CHUNKS)
        for direction in (step_up, step_down):
            side, step, origin, edge, via, target = direction

            @pl.when(edge)
            def _():
                onward = remote(
                    relay.at[index], slabs.at[2 * side, t, :, block(source), :], y_send.at[k, t, side],
                    y_recv.at[k, t, side], {"lat": target},
                )
                remote(part_of(t), relay.at[index], y_send.at[k, t, side], r_recv.at[index], {"lat": via}).wait_recv()
                onward.start()

    def part_of(t):
        return sends.at[zone, t]

    def rows_arrived():
        for k in range(CHUNKS):
            for t in range(TILES):

                @pl.when(jnp.logical_not(edge_low))
                def _():
                    row_copy(k, t, step_up).wait_recv()

                @pl.when(jnp.logical_not(edge_high))
                def _():
                    row_copy(k, t, step_down).wait_recv()

    def rows_sent():
        for k in range(CHUNKS):
            for t in range(TILES):
                for direction in (step_up, step_down):
                    if (k, t) in relayed:
                        row_copy(k, t, direction).wait_send()
                    else:

                        @pl.when(jnp.logical_not(direction[3]))
                        def _():
                            row_copy(k, t, direction).wait_send()

    def pass_far(k):
        source = lax.rem(zone - k + CHUNKS, CHUNKS)
        for side, row, step in ((0, ROWS - 1, 2), (1, 0, -2)):
            for half in range(2):
                src = slabs.at[1, :, :, pl.ds(16 * source + 8 * half + row, 1), :]
                dst = far.at[side, :, :, pl.ds(2 * source + half, 1), :]
                copy = remote(src, dst, f_send.at[k, side, half], f_recv.at[k, side, half], lat_peer(step))
                copy.start()
                far_copies.append(copy)

    load_m.wait()
    for t in range(TILES):

        def member_chunks(lev, carry, t=t):
            half = lev // HALF
            place = jnp.where(half == 0, lev, LEV - 1 - lev)
            tiles = lane_tiles(xm, lev)
            for part in range(CHUNKS):
                sends[part, t, place, pl.ds(pl.multiple_of(8 * half, 8), 8), :] = chunk_tile(tiles, part, t)
            return carry

        lax.fori_loop(0, LEV, member_chunks, 0)
        if t == 0:
            pl.semaphore_wait(barrier, len(partners) + 31)
        for k in (1, 3):
            zone_copies[k, t].start()
        pass_on(0, t)
        local_copies[t].start()

    load_c.wait()
    for part in range(CHUNKS):

        @pl.when(zone == part)
        def _(part=part):
            def cond_chunk(lev, carry):
                place = jnp.where(lev < HALF, lev, HALF + LEV - 1 - lev)
                tiles = lane_tiles(xc, lev)
                for t in range(TILES):
                    cond[1, place, t] = chunk_tile(tiles, part, t)
                return carry

            lax.fori_loop(0, LEV, cond_chunk, 0)

    own_half = pl.ds(pl.multiple_of(HALF * core, HALF), HALF)
    far_up = (cond.at[1, own_half, :, pl.ds(7, 1), :], cond_far.at[0, own_half, :, pl.ds(0, 1), :])
    far_down = (cond.at[1, own_half, :, pl.ds(0, 1), :], cond_far.at[1, own_half, :, pl.ds(0, 1), :])
    cond_copies = [
        remote(cond.at[1, own_half], cond.at[0, own_half], c_send.at[0], c_recv.at[0], lat_peer(1)),
        remote(cond.at[1, own_half], cond.at[2, own_half], c_send.at[1], c_recv.at[1], lat_peer(-1)),
        remote(*far_up, c_send.at[2], c_recv.at[2], lat_peer(2)),
        remote(*far_down, c_send.at[3], c_recv.at[3], lat_peer(-2)),
    ]
    for copy in cond_copies:
        copy.start()
    for t in range(TILES):
        zone_copies[2, t].start()
    weight_own[...] = jnp.full((8, 128), weights[0], jnp.float32)
    weight_copies = [
        remote(weight_own, weight_in.at[k - 1], w_send.at[k - 1], w_recv.at[k - 1], zone_peer(k)) for k in (1, 2, 3)
    ]
    for copy in weight_copies:
        copy.start()
    for slab, edge in ((0, edge_low), (2, edge_high)):

        @pl.when(edge)
        def _(slab=slab):
            def clear(place, carry):
                for t in range(TILES):
                    slabs[slab, t, place] = jnp.zeros((64, 128), jnp.float32)
                return carry

            lax.fori_loop(0, HALF, clear, 0)

    for copy in local_copies:
        copy.wait()
    pass_far(0)

    sub = lax.broadcasted_iota(jnp.int32, (8, 128), 0)
    even = sub % 2 == 0

    def spread(low, high):
        return jnp.where(even, jnp.broadcast_to(low, (8, 128)), jnp.broadcast_to(high, (8, 128)))

    def swap_halves(value):
        return jnp.where(even, pltpu.roll(value, 7, 0), pltpu.roll(value, 1, 0))

    def sides(value):
        west, east = pltpu.roll(value[2], 1, 1), pltpu.roll(value[0], 127, 1)
        return [west + value[1], value[0] + value[2], value[1] + east]

    def stencil(src, row, place):
        value = [src[row, place, t] for t in range(TILES)]
        total = sides(value)
        for t in range(TILES):
            total[t] = total[t] + (src[row - 1, place, t] + src[row + 1, place, t])
            if place > 0:
                total[t] = total[t] + src[row, place - 1, t]
            total[t] = total[t] + (src[row, place + 1, t] if place < HALF - 1 else swap_halves(value[t]))
        return value, total

    inside_low = jnp.where(lat == 0, 0.0, 1.0)
    inside_high = jnp.where(lat == lat_count - 1, 0.0, 1.0)
    far_low = jnp.where(lat <= 1, 0.0, 1.0)
    far_high = jnp.where(lat >= lat_count - 2, 0.0, 1.0)

    def root_rows(ref, source, count, first, inside):
        def body(row, carry):
            for place in range(HALF):
                for t in range(TILES):
                    low = ref[source, place, t, pl.ds(row, 1), :]
                    high = ref[source, HALF + place, t, pl.ds(row, 1), :]
                    table_s[first + row, place, t] = jnp.sqrt(spread(low, high)) * inside
            return carry

        lax.fori_loop(0, count, body, 0)

    def table_rows(low, high):
        def body(row, carry):
            for place in range(HALF):
                value, total = stencil(table_s, row, place)
                for t in range(TILES):
                    table_d[row, place, t] = 1.0 - STEP * (value[t] * total[t])
                    table_g[row, place, t] = STEP * (value[t] * value[t])
            return carry

        lax.fori_loop(low, high, body, 0)

    def start_rows(slab, first):
        def body(row, carry):
            for place in range(HALF):
                for t in range(TILES):
                    value = slabs[slab, t, place, pl.ds(row, 8, stride=8), :]
                    start[first + row, place, t] = value * table_s[first + row, place, t]
            return carry

        lax.fori_loop(0, ROWS, body, 0)

    root_rows(cond, 1, ROWS, OWN, 1.0)
    for k in (1, 3):
        zone_copies[k, 0].wait_recv()
        pass_on(k, 0)
    for copy in cond_copies:
        copy.wait()
    hand_copies = [
        remote(cond.at[0, own_half], cond.at[0, own_half], c_send.at[4], c_recv.at[4], sibling),
        remote(cond.at[2, own_half], cond.at[2, own_half], c_send.at[5], c_recv.at[5], sibling),
        remote(cond_far.at[:, own_half], cond_far.at[:, own_half], c_send.at[6], c_recv.at[6], sibling),
    ]
    for copy in hand_copies:
        copy.start()
    relay_on(0, 0)
    for k in (1, 3):
        zone_copies[k, 1].wait_recv()
        pass_on(k, 1)
    for copy in hand_copies:
        copy.wait()
    root_rows(cond, 0, ROWS, OWN - ROWS, inside_low)
    root_rows(cond, 2, ROWS, OWN + ROWS, inside_high)
    root_rows(cond_far, 0, 1, 0, far_low)
    root_rows(cond_far, 1, 1, ALL - 1, far_high)
    for k in (1, 3):
        zone_copies[k, 2].wait_recv()
        pass_on(k, 2)
        pass_far(k)
        relay_on(k, 0)
    table_rows(1, ALL // 2)
    zone_copies[2, 0].wait_recv()
    pass_on(2, 0)
    relay_on(1, 1)
    table_rows(ALL // 2, ALL - 1)
    for t in range(1, TILES):
        zone_copies[2, t].wait_recv()
        pass_on(2, t)
    pass_far(2)
    relay_on(3, 2)
    relay_on(2, 0)
    start_rows(1, OWN)
    for copy in weight_copies:
        copy.wait()
    group = sub // 2
    weight = jnp.zeros((8, 128), jnp.float32)
    total_weight = weight_own[...]
    for k in range(CHUNKS):
        value = weight_own[...] if k == 0 else weight_in[k - 1]
        weight = jnp.where(group == lax.rem(zone - k + CHUNKS, CHUNKS), value, weight)
        if k > 0:
            total_weight = total_weight + value
    weight_sum[...] = total_weight

    rows_arrived()
    start_rows(0, OWN - ROWS)
    start_rows(2, OWN + ROWS)
    for copy in far_copies:
        copy.wait_recv()
    for side, row in ((0, 0), (1, ALL - 1)):
        for place in range(HALF):
            for t in range(TILES):
                start[row, place, t] = far[side, t, place] * table_s[row, place, t]

    def heat(src, dst, index):
        low = (index - 1) // 2 * 2 + 1

        def rows(j, carry):
            for place in range(HALF):
                for r in range(4):
                    row = low + 4 * j + r
                    value, total = stencil(src, row, place)
                    for t in range(TILES):
                        dst[row, place, t] = table_d[row, place, t] * value[t] + table_g[row, place, t] * total[t]
            return carry

        lax.fori_loop(0, (ALL - 2 * low) // 4, rows, 0)

    def guarded(value):
        return jnp.where(value > 0.0, value, 1.0)

    upper = sub >= 4
    odd_pair = (sub // 2) % 2 == 1

    def fold(a, b, c, d):
        def halves(x, y):
            return jnp.where(upper, y, x) + pltpu.roll(jnp.where(upper, x, y), 4, 0)

        x, y = halves(a, c), halves(b, d)
        other = jnp.where(odd_pair, pltpu.roll(y, 2, 0), pltpu.roll(x, 6, 0))
        return jnp.where(odd_pair, y, x) + other

    def log_sums(row, q, t):
        return fold(*[weight * jnp.log(guarded(buf_a[row, 4 * q + j, t])) for j in range(4)])

    heat(start, buf_a, 1)
    heat(buf_a, buf_b, 2)
    heat(buf_b, buf_a, 3)

    def first_logs(i, carry):
        for q in range(2):
            for t in range(TILES):
                logs[i, q, t] = log_sums(i + PASSES, q, t)
        return carry

    mid = INNER // 2
    sibling_copies = [
        remote(weight_sum, weight_other, s_send.at[0], s_recv.at[0], sibling),
        remote(logs.at[pl.ds(0, mid)], logs_other.at[pl.ds(0, mid)], s_send.at[1], s_recv.at[1], sibling),
        remote(logs.at[pl.ds(mid, mid)], logs_other.at[pl.ds(mid, mid)], s_send.at[2], s_recv.at[2], sibling),
    ]
    sibling_copies[0].start()
    lax.fori_loop(0, mid, first_logs, 0)
    sibling_copies[1].start()
    lax.fori_loop(mid, INNER, first_logs, 0)
    sibling_copies[2].start()
    sibling_copies[0].wait()
    inverse = 1.0 / (weight_sum[...] + weight_other[...])

    def rescale(i, carry):
        row = i + PASSES
        for q in range(2):
            for t in range(TILES):
                logs_other[i, q, t] = jnp.exp((logs[i, q, t] + logs_other[i, q, t]) * inverse)
        for place in range(HALF):
            q, j = place // 4, place % 4
            for t in range(TILES):
                power = spread(logs_other[i, q, t, pl.ds(2 * j, 1), :], logs_other[i, q, t, pl.ds(2 * j + 1, 1), :])
                buf_b[row, place, t] = table_s[row, place, t] * power / guarded(buf_a[row, place, t])
        return carry

    sibling_copies[1].wait()
    lax.fori_loop(0, mid, rescale, 0)
    sibling_copies[2].wait()
    lax.fori_loop(mid, INNER, rescale, 0)
    heat(buf_b, buf_a, 4)
    heat(buf_a, buf_b, 5)
    heat(buf_b, buf_a, 6)

    def ratio(row, carry):
        for place in range(HALF):
            for t in range(TILES):
                top = start[row, place, t] * table_s[row, place, t]
                buf_b[row, place, t] = top / guarded(buf_a[row, place, t])
        return carry

    lax.fori_loop(2 * PASSES, ALL - 2 * PASSES, ratio, 0)
    heat(buf_b, buf_a, 7)
    heat(buf_a, buf_b, 8)
    heat(buf_b, buf_a, 9)

    def second_logs(i, carry):
        for q in range(2):
            for t in range(TILES):
                final[t, q, pl.ds(pl.multiple_of(8 * i, 8), 8), :] = log_sums(i + OWN, q, t)
        return carry

    lax.fori_loop(0, ROWS, second_logs, 0)
    final_copy = remote(final, final_other, s_send.at[3], s_recv.at[3], sibling)
    final_copy.start()
    final_copy.wait()
    valid = []
    for t in range(TILES):
        at = 3 * lanes() + t
        valid.append((at >= GHOST) & (at < GHOST + COLS))
    summed = jnp.zeros((8, 128), jnp.float32)
    for lev in range(LEV):
        half, place = (0, lev) if lev < HALF else (1, LEV - 1 - lev)
        across = pl.ds(2 * (place % 4) + half, 8, stride=8)
        for t in range(TILES):
            value = jnp.exp((final[t, place // 4, across, :] + final_other[t, place // 4, across, :]) * inverse)
            value = value * lax.rsqrt(cond[1, HALF * half + place, t])
            summed = summed + jnp.where(valid[t], value, 0.0)
            shares[lev // 4, lev // 2 % 2, lev % 2, t] = value

    mass[0] = summed
    column_copies = [
        remote(mass.at[0], column_in.at[k - 1], t_send.at[k - 1], t_recv.at[k - 1], column_peer(k)) for k in range(1, 8)
    ]
    for copy in column_copies:
        copy.start()
    share_copies = [
        remote(
            shares.at[lax.rem(zone + k, CHUNKS), core], gathered.at[zone], g_send.at[k - 1], g_recv.at[k - 1],
            zone_peer(k),
        )
        for k in (1, 2, 3)
    ]
    for copy in share_copies:
        copy.start()
    gathered[zone] = shares[zone, core]
    for k, copy in enumerate(column_copies):
        copy.wait()
        summed = summed + column_in[k]

    mass[1] = summed

    def plane_copy(k):
        return remote(mass.at[1], plane_in.at[k - 1], p_send.at[k - 1], p_recv.at[k - 1], plane_peer(k))

    def send_plane(k, carry):
        plane_copy(k).start()
        return carry

    lax.fori_loop(1, 32, send_plane, 0)
    for copy in share_copies:
        copy.wait()
    joined = []
    for i in range(2):
        chunks = [[gathered[part, i, t] for t in range(TILES)] for part in range(CHUNKS)]
        joined.append([joined_tile(chunks, index) for index in range(12)])
    for t in range(TILES):
        for k in (1, 2, 3):
            zone_copies[k, t].wait_send()
    rows_sent()
    for copy in far_copies:
        copy.wait_send()

    def take_plane(k, value):
        plane_copy(k).wait()
        return value + plane_in[k - 1]

    summed = lax.fori_loop(1, 32, take_plane, summed)
    cells = LEV * ROWS * lat_count * LON
    scale = cells / jnp.sum(summed)
    for i in range(2):
        for index in range(11):
            out[i, :, pl.ds(128 * index, 128)] = joined[i][index] * scale
        out[i, :, pl.ds(LAST, LON - LAST)] = (joined[i][11] * scale)[:, : LON - LAST]


def local(members, conductivity, weights):
    vmem = functools.partial(pltpu.VMEM, dtype=jnp.float32)
    dma = pltpu.SemaphoreType.DMA
    tiled = (TILES, 8, 128)
    table = (ALL, HALF) + tiled
    return pl.pallas_call(
        kernel,
        name="barycenter",
        out_shape=jax.ShapeDtypeStruct((2, ROWS, LON), jnp.float32),
        in_specs=[
            pl.BlockSpec(memory_space=pl.ANY),
            pl.BlockSpec(memory_space=pl.ANY),
            pl.BlockSpec(memory_space=pltpu.SMEM),
        ],
        out_specs=pl.BlockSpec(memory_space=pltpu.VMEM),
        scratch_shapes=[
            vmem((LEV, ROWS, LON)),
            vmem((LEV, ROWS, LON)),
            vmem((CHUNKS, TILES, HALF, 16, 128)),
            vmem((3, TILES, HALF, 64, 128)),
            vmem((6, HALF, 16, 128)),
            vmem((2, TILES, HALF, 8, 128)),
            vmem((3, LEV) + tiled),
            vmem((2, LEV) + tiled),
            vmem(table), vmem(table), vmem(table),
            vmem(table), vmem(table), vmem(table),
            vmem((INNER, 2) + tiled),
            vmem((INNER, 2) + tiled),
            vmem((TILES, 2, 64, 128)),
            vmem((TILES, 2, 64, 128)),
            vmem((CHUNKS, 2, 2) + tiled),
            vmem((CHUNKS, 2) + tiled),
            vmem((8, 128)),
            vmem((3, 8, 128)),
            vmem((8, 128)),
            vmem((8, 128)),
            vmem((2, 8, 128)),
            vmem((7, 8, 128)),
            vmem((31, 8, 128)),
            dma((2,)), dma((3,)), dma((6,)),
            dma((3, 3)), dma((3, 3)), dma((3,)), dma((3,)), dma((7,)), dma((7,)),
            dma((4, 3, 2)), dma((4, 3, 2)), dma((4, 2, 2)), dma((4, 2, 2)), dma((4,)), dma((4,)),
            dma((3,)), dma((3,)), dma((7,)), dma((7,)), dma((31,)), dma((31,)),
        ],
        compiler_params=pltpu.CompilerParams(
            collective_id=0, has_side_effects=True, vmem_limit_bytes=60 * 1024 * 1024
        ),
    )(members, conductivity, weights)


def solution(mesh):
    placed = (P("member", None, "lat", None), P(None, "lat", None), P("member"))
    return jax.shard_map(
        local, mesh=mesh, in_specs=placed, out_specs=P("member", "lat", None), check_vma=False
    )
```

```python
import functools

import jax
import jax.numpy as jnp
from jax import lax
from jax.experimental import pallas as pl
from jax.experimental.pallas import tpu as pltpu
from jax.sharding import PartitionSpec as P

MESH = pl.DeviceIdType.MESH
STEP = 0.16
PASSES = 3
LEV, ROWS, LON = 16, 8, 1440
HALF = LEV // 2
CHUNKS = 4
COLS = LON // CHUNKS
GHOST = 12
TILES = 3
HALO = 3 * PASSES
ALL = ROWS + 2 * HALO
OWN = HALO
INNER = ROWS + 4 * PASSES
LAST = 1408


def lanes():
    return lax.broadcasted_iota(jnp.int32, (8, 128), 1)


def lane_tiles(ref, lev):
    tiles = [ref[lev, :, pl.ds(128 * i, 128)] for i in range(11)]
    return tiles + [jnp.concatenate([ref[lev, :, pl.ds(LAST, LON - LAST)], tiles[0][:, : 128 - (LON - LAST)]], axis=1)]


def chunk_tile(tiles, part, t):
    lane = lanes()
    start = COLS * part - GHOST
    shift = start % 128
    at = shift + 3 * lane + t
    if part == 0:
        window = [tiles[11], tiles[0], tiles[1], tiles[2]]
        index = jnp.where(at < 128, at - 96, at % 128)
        edges = [128, 256, 384]
    else:
        window = [tiles[start // 128 + i] for i in range(4)]
        index = at % 128
        edges = [128, 256, 384]
        if part == CHUNKS - 1:
            window.append(tiles[0])
            wrap = LON - 128 * (start // 128)
            index = jnp.where(at >= wrap, at - wrap, index)
            edges.append(wrap)
    value = jnp.take_along_axis(window[0], index, axis=1)
    for piece, edge in zip(window[1:], edges):
        value = jnp.where(at >= edge, jnp.take_along_axis(piece, index, axis=1), value)
    return value


def joined_tile(chunks, index):
    lane = lanes()
    result = None
    for part in range(CHUNKS):
        low, high = COLS * part, COLS * (part + 1)
        if low >= 128 * (index + 1) or high <= 128 * index:
            continue
        column = 128 * index + lane - low + GHOST
        source = jnp.clip(column // 3, 0, 127)
        kind = column % 3
        pieces = [jnp.take_along_axis(chunks[part][t], source, axis=1) for t in range(TILES)]
        value = jnp.where(kind == 0, pieces[0], jnp.where(kind == 1, pieces[1], pieces[2]))
        result = value if result is None else jnp.where(lane < low - 128 * index, result, value)
    return result


def kernel(
    members, conductivity, weights, out,
    xm, xc, sends, slabs, relay, far, cond, cond_far, table_s, table_d, table_g, start, buf_a, buf_b,
    logs, logs_other, final, final_other, shares, gathered,
    weight_own, weight_in, weight_sum, weight_other, mass, column_in, plane_in,
    load_sem, local_sem, r_recv, z_send, z_recv, w_send, w_recv, c_send, c_recv, y_send, y_recv, f_send, f_recv,
    s_send, s_recv, g_send, g_recv, t_send, t_recv, p_send, p_recv,
):
    me = lax.axis_index("member")
    lat = lax.axis_index("lat")
    zone, core = me // 2, lax.rem(me, 2)
    lat_count = lax.axis_size("lat")

    def zone_peer(k):
        return {"member": lax.rem(zone + k, CHUNKS) * 2 + core}

    def lat_peer(k):
        return {"lat": lax.rem(lat + k + lat_count, lat_count)}

    sibling = {"member": me + 1 - 2 * core}

    def column_peer(k):
        place = lax.rem(2 * zone + lat // 32 + k, 8)
        return {"member": place // 2 * 2 + core, "lat": lax.rem(place, 2) * 32 + lax.rem(lat, 32)}

    def plane_peer(k):
        return {"lat": lat // 32 * 32 + lax.rem(lat + k, 32)}

    load_m = pltpu.make_async_copy(members.at[0], xm, load_sem.at[1])
    load_c = pltpu.make_async_copy(conductivity, xc, load_sem.at[0])
    load_m.start()
    load_c.start()

    barrier = pltpu.get_barrier_semaphore()
    partners = [lat_peer(k) for k in (1, -1, 2, -2)] + [sibling] + [column_peer(k) for k in range(1, 8)]
    for partner in partners:
        pl.semaphore_signal(barrier, inc=1, device_id=partner, device_id_type=MESH)

    def greet(k, carry):
        pl.semaphore_signal(barrier, inc=1, device_id=plane_peer(k), device_id_type=MESH)
        return carry

    lax.fori_loop(1, 32, greet, 0)

    def remote(src, dst, send, recv, target):
        return pltpu.make_async_remote_copy(
            src_ref=src, dst_ref=dst, send_sem=send, recv_sem=recv, device_id=target, device_id_type=MESH
        )

    def block(b):
        return pl.ds(pl.multiple_of(16 * b, 16), 16)

    zone_copies = {
        (k, t): remote(
            sends.at[lax.rem(zone + k, CHUNKS), t], slabs.at[1, t, :, block(zone), :],
            z_send.at[k - 1, t], z_recv.at[k - 1, t], zone_peer(k),
        )
        for k in (1, 3, 2)
        for t in range(TILES)
    }
    local_copies = [
        pltpu.make_async_copy(sends.at[zone, t], slabs.at[1, t, :, block(zone), :], local_sem.at[t])
        for t in range(TILES)
    ]
    far_copies = []
    edge_low, edge_high = lat == 0, lat == lat_count - 1
    middle = lat_count // 2
    relayed = {(k, t): 2 * k + t for k in range(CHUNKS) for t in range(2)}
    step_up = (0, 1, middle - 1, edge_high, lat_count - 1, middle)
    step_down = (1, -1, middle, edge_low, 0, middle - 1)

    def row_copy(k, t, direction):
        side, step = direction[0], direction[1]
        source = lax.rem(zone - k + CHUNKS, CHUNKS)
        part = sends.at[zone, t] if k == 0 else slabs.at[1, t, :, block(source), :]
        return remote(
            part, slabs.at[2 * side, t, :, block(source), :], y_send.at[k, t, side], y_recv.at[k, t, side], lat_peer(step)
        )

    def pass_on(k, t):
        source = lax.rem(zone - k + CHUNKS, CHUNKS)
        part = sends.at[zone, t] if k == 0 else slabs.at[1, t, :, block(source), :]
        for direction in (step_up, step_down):
            side, step, origin, edge, via, target = direction
            if (k, t) in relayed:
                index = relayed[k, t]

                @pl.when((lat != origin) & jnp.logical_not(edge))
                def _():
                    row_copy(k, t, direction).start()

                @pl.when(lat == origin)
                def _():
                    remote(part, relay.at[index], y_send.at[k, t, side], r_recv.at[index], {"lat": via}).start()

            else:

                @pl.when(jnp.logical_not(edge))
                def _():
                    row_copy(k, t, direction).start()

    def relay_on(k, t):
        if (k, t) not in relayed:
            return
        index = relayed[k, t]
        source = lax.rem(zone - k + CHUNKS, CHUNKS)
        for direction in (step_up, step_down):
            side, step, origin, edge, via, target = direction

            @pl.when(edge)
            def _():
                onward = remote(
                    relay.at[index], slabs.at[2 * side, t, :, block(source), :], y_send.at[k, t, side],
                    y_recv.at[k, t, side], {"lat": target},
                )
                remote(part_of(t), relay.at[index], y_send.at[k, t, side], r_recv.at[index], {"lat": via}).wait_recv()
                onward.start()

    def part_of(t):
        return sends.at[zone, t]

    def rows_arrived(direction, edge):
        for k in range(CHUNKS):
            for t in range(TILES):

                @pl.when(jnp.logical_not(edge))
                def _():
                    row_copy(k, t, direction).wait_recv()

    def rows_sent():
        for k in range(CHUNKS):
            for t in range(TILES):
                for direction in (step_up, step_down):
                    if (k, t) in relayed:
                        row_copy(k, t, direction).wait_send()
                    else:

                        @pl.when(jnp.logical_not(direction[3]))
                        def _():
                            row_copy(k, t, direction).wait_send()

    def pass_far(k):
        source = lax.rem(zone - k + CHUNKS, CHUNKS)
        for side, row, step in ((0, ROWS - 1, 2), (1, 0, -2)):
            for half in range(2):
                src = slabs.at[1, :, :, pl.ds(16 * source + 8 * half + row, 1), :]
                dst = far.at[side, :, :, pl.ds(2 * source + half, 1), :]
                copy = remote(src, dst, f_send.at[k, side, half], f_recv.at[k, side, half], lat_peer(step))
                copy.start()
                far_copies.append(copy)

    load_m.wait()
    for t in range(TILES):

        def member_chunks(lev, carry, t=t):
            half = lev // HALF
            place = jnp.where(half == 0, lev, LEV - 1 - lev)
            tiles = lane_tiles(xm, lev)
            for part in range(CHUNKS):
                sends[part, t, place, pl.ds(pl.multiple_of(8 * half, 8), 8), :] = chunk_tile(tiles, part, t)
            return carry

        lax.fori_loop(0, LEV, member_chunks, 0)
        if t == 0:
            pl.semaphore_wait(barrier, len(partners) + 31)
        for k in (1, 3):
            zone_copies[k, t].start()
        pass_on(0, t)
        local_copies[t].start()

    load_c.wait()
    for part in range(CHUNKS):

        @pl.when(zone == part)
        def _(part=part):
            def cond_chunk(lev, carry):
                place = jnp.where(lev < HALF, lev, HALF + LEV - 1 - lev)
                tiles = lane_tiles(xc, lev)
                for t in range(TILES):
                    cond[1, place, t] = chunk_tile(tiles, part, t)
                return carry

            lax.fori_loop(0, LEV, cond_chunk, 0)

    own_half = pl.ds(pl.multiple_of(HALF * core, HALF), HALF)
    far_up = (cond.at[1, own_half, :, pl.ds(7, 1), :], cond_far.at[0, own_half, :, pl.ds(0, 1), :])
    far_down = (cond.at[1, own_half, :, pl.ds(0, 1), :], cond_far.at[1, own_half, :, pl.ds(0, 1), :])
    cond_copies = [
        remote(cond.at[1, own_half], cond.at[0, own_half], c_send.at[0], c_recv.at[0], lat_peer(1)),
        remote(cond.at[1, own_half], cond.at[2, own_half], c_send.at[1], c_recv.at[1], lat_peer(-1)),
        remote(*far_up, c_send.at[2], c_recv.at[2], lat_peer(2)),
        remote(*far_down, c_send.at[3], c_recv.at[3], lat_peer(-2)),
    ]
    for copy in cond_copies:
        copy.start()
    for t in range(TILES):
        zone_copies[2, t].start()
    weight_own[...] = jnp.full((8, 128), weights[0], jnp.float32)
    weight_copies = [
        remote(weight_own, weight_in.at[k - 1], w_send.at[k - 1], w_recv.at[k - 1], zone_peer(k)) for k in (1, 2, 3)
    ]
    for copy in weight_copies:
        copy.start()
    for slab, edge in ((0, edge_low), (2, edge_high)):

        @pl.when(edge)
        def _(slab=slab):
            def clear(place, carry):
                for t in range(TILES):
                    slabs[slab, t, place] = jnp.zeros((64, 128), jnp.float32)
                return carry

            lax.fori_loop(0, HALF, clear, 0)

    for copy in local_copies:
        copy.wait()
    pass_far(0)

    sub = lax.broadcasted_iota(jnp.int32, (8, 128), 0)
    even = sub % 2 == 0

    def spread(low, high):
        return jnp.where(even, jnp.broadcast_to(low, (8, 128)), jnp.broadcast_to(high, (8, 128)))

    def swap_halves(value):
        return jnp.where(even, pltpu.roll(value, 7, 0), pltpu.roll(value, 1, 0))

    def sides(value):
        west, east = pltpu.roll(value[2], 1, 1), pltpu.roll(value[0], 127, 1)
        return [west + value[1], value[0] + value[2], value[1] + east]

    def stencil(src, row, place):
        value = [src[row, place, t] for t in range(TILES)]
        total = sides(value)
        for t in range(TILES):
            total[t] = total[t] + (src[row - 1, place, t] + src[row + 1, place, t])
            if place > 0:
                total[t] = total[t] + src[row, place - 1, t]
            total[t] = total[t] + (src[row, place + 1, t] if place < HALF - 1 else swap_halves(value[t]))
        return value, total

    inside_low = jnp.where(lat == 0, 0.0, 1.0)
    inside_high = jnp.where(lat == lat_count - 1, 0.0, 1.0)
    far_low = jnp.where(lat <= 1, 0.0, 1.0)
    far_high = jnp.where(lat >= lat_count - 2, 0.0, 1.0)

    def root_rows(ref, source, count, first, inside):
        def body(row, carry):
            for place in range(HALF):
                for t in range(TILES):
                    low = ref[source, place, t, pl.ds(row, 1), :]
                    high = ref[source, HALF + place, t, pl.ds(row, 1), :]
                    table_s[first + row, place, t] = jnp.sqrt(spread(low, high)) * inside
            return carry

        lax.fori_loop(0, count, body, 0)

    def table_rows(low, high):
        def body(row, carry):
            for place in range(HALF):
                value, total = stencil(table_s, row, place)
                for t in range(TILES):
                    table_d[row, place, t] = 1.0 - STEP * (value[t] * total[t])
                    table_g[row, place, t] = STEP * (value[t] * value[t])
            return carry

        lax.fori_loop(low, high, body, 0)

    def start_rows(slab, first):
        def body(row, carry):
            for place in range(HALF):
                for t in range(TILES):
                    value = slabs[slab, t, place, pl.ds(row, 8, stride=8), :]
                    start[first + row, place, t] = value * table_s[first + row, place, t]
            return carry

        lax.fori_loop(0, ROWS, body, 0)

    root_rows(cond, 1, ROWS, OWN, 1.0)
    for k in (1, 3):
        zone_copies[k, 0].wait_recv()
        pass_on(k, 0)
    for copy in cond_copies:
        copy.wait()
    hand_copies = [
        remote(cond.at[0, own_half], cond.at[0, own_half], c_send.at[4], c_recv.at[4], sibling),
        remote(cond.at[2, own_half], cond.at[2, own_half], c_send.at[5], c_recv.at[5], sibling),
        remote(cond_far.at[:, own_half], cond_far.at[:, own_half], c_send.at[6], c_recv.at[6], sibling),
    ]
    for copy in hand_copies:
        copy.start()
    for t in range(TILES):
        relay_on(0, t)
    for k in (1, 3):
        zone_copies[k, 1].wait_recv()
        pass_on(k, 1)
    for copy in hand_copies:
        copy.wait()
    root_rows(cond, 0, ROWS, OWN - ROWS, inside_low)
    root_rows(cond, 2, ROWS, OWN + ROWS, inside_high)
    root_rows(cond_far, 0, 1, 0, far_low)
    root_rows(cond_far, 1, 1, ALL - 1, far_high)
    for k in (1, 3):
        zone_copies[k, 2].wait_recv()
        pass_on(k, 2)
        pass_far(k)
        relay_on(k, 0)
        relay_on(k, 1)
    table_rows(1, ALL // 2)
    zone_copies[2, 0].wait_recv()
    pass_on(2, 0)
    relay_on(1, 2)
    relay_on(3, 2)
    table_rows(ALL // 2, ALL - 1)
    for t in range(1, TILES):
        zone_copies[2, t].wait_recv()
        pass_on(2, t)
    pass_far(2)
    for t in range(TILES):
        relay_on(2, t)
    start_rows(1, OWN)
    for copy in weight_copies:
        copy.wait()
    group = sub // 2
    weight = jnp.zeros((8, 128), jnp.float32)
    total_weight = weight_own[...]
    for k in range(CHUNKS):
        value = weight_own[...] if k == 0 else weight_in[k - 1]
        weight = jnp.where(group == lax.rem(zone - k + CHUNKS, CHUNKS), value, weight)
        if k > 0:
            total_weight = total_weight + value
    weight_sum[...] = total_weight

    rows_arrived(step_up, edge_low)
    start_rows(0, OWN - ROWS)
    rows_arrived(step_down, edge_high)
    start_rows(2, OWN + ROWS)
    for copy in far_copies:
        copy.wait_recv()
    for side, row in ((0, 0), (1, ALL - 1)):
        for place in range(HALF):
            for t in range(TILES):
                start[row, place, t] = far[side, t, place] * table_s[row, place, t]

    def heat(src, dst, index):
        low = (index - 1) // 2 * 2 + 1

        def rows(j, carry):
            for place in range(HALF):
                for r in range(4):
                    row = low + 4 * j + r
                    value, total = stencil(src, row, place)
                    for t in range(TILES):
                        dst[row, place, t] = table_d[row, place, t] * value[t] + table_g[row, place, t] * total[t]
            return carry

        lax.fori_loop(0, (ALL - 2 * low) // 4, rows, 0)

    def guarded(value):
        return jnp.where(value > 0.0, value, 1.0)

    upper = sub >= 4
    odd_pair = (sub // 2) % 2 == 1

    def fold(a, b, c, d):
        def halves(x, y):
            return jnp.where(upper, y, x) + pltpu.roll(jnp.where(upper, x, y), 4, 0)

        x, y = halves(a, c), halves(b, d)
        other = jnp.where(odd_pair, pltpu.roll(y, 2, 0), pltpu.roll(x, 6, 0))
        return jnp.where(odd_pair, y, x) + other

    def log_sums(row, q, t):
        return fold(*[weight * jnp.log(guarded(buf_a[row, 4 * q + j, t])) for j in range(4)])

    heat(start, buf_a, 1)
    heat(buf_a, buf_b, 2)
    heat(buf_b, buf_a, 3)

    def first_logs(i, carry):
        for q in range(2):
            for t in range(TILES):
                logs[i, q, t] = log_sums(i + PASSES, q, t)
        return carry

    mid = INNER // 2
    sibling_copies = [
        remote(weight_sum, weight_other, s_send.at[0], s_recv.at[0], sibling),
        remote(logs.at[pl.ds(0, mid)], logs_other.at[pl.ds(0, mid)], s_send.at[1], s_recv.at[1], sibling),
        remote(logs.at[pl.ds(mid, mid)], logs_other.at[pl.ds(mid, mid)], s_send.at[2], s_recv.at[2], sibling),
    ]
    sibling_copies[0].start()
    lax.fori_loop(0, mid, first_logs, 0)
    sibling_copies[1].start()
    lax.fori_loop(mid, INNER, first_logs, 0)
    sibling_copies[2].start()
    sibling_copies[0].wait()
    inverse = 1.0 / (weight_sum[...] + weight_other[...])

    def rescale(i, carry):
        row = i + PASSES
        for q in range(2):
            for t in range(TILES):
                logs_other[i, q, t] = jnp.exp((logs[i, q, t] + logs_other[i, q, t]) * inverse)
        for place in range(HALF):
            q, j = place // 4, place % 4
            for t in range(TILES):
                power = spread(logs_other[i, q, t, pl.ds(2 * j, 1), :], logs_other[i, q, t, pl.ds(2 * j + 1, 1), :])
                buf_b[row, place, t] = table_s[row, place, t] * power / guarded(buf_a[row, place, t])
        return carry

    sibling_copies[1].wait()
    lax.fori_loop(0, mid, rescale, 0)
    sibling_copies[2].wait()
    lax.fori_loop(mid, INNER, rescale, 0)
    heat(buf_b, buf_a, 4)
    heat(buf_a, buf_b, 5)
    heat(buf_b, buf_a, 6)

    def ratio(row, carry):
        for place in range(HALF):
            for t in range(TILES):
                top = start[row, place, t] * table_s[row, place, t]
                buf_b[row, place, t] = top / guarded(buf_a[row, place, t])
        return carry

    lax.fori_loop(2 * PASSES, ALL - 2 * PASSES, ratio, 0)
    heat(buf_b, buf_a, 7)
    heat(buf_a, buf_b, 8)
    heat(buf_b, buf_a, 9)

    def second_logs(i, carry):
        for q in range(2):
            for t in range(TILES):
                final[t, q, pl.ds(pl.multiple_of(8 * i, 8), 8), :] = log_sums(i + OWN, q, t)
        return carry

    lax.fori_loop(0, ROWS, second_logs, 0)
    final_copy = remote(final, final_other, s_send.at[3], s_recv.at[3], sibling)
    final_copy.start()
    final_copy.wait()
    valid = []
    for t in range(TILES):
        at = 3 * lanes() + t
        valid.append((at >= GHOST) & (at < GHOST + COLS))
    summed = jnp.zeros((8, 128), jnp.float32)
    for lev in range(LEV):
        half, place = (0, lev) if lev < HALF else (1, LEV - 1 - lev)
        across = pl.ds(2 * (place % 4) + half, 8, stride=8)
        for t in range(TILES):
            value = jnp.exp((final[t, place // 4, across, :] + final_other[t, place // 4, across, :]) * inverse)
            value = value * lax.rsqrt(cond[1, HALF * half + place, t])
            summed = summed + jnp.where(valid[t], value, 0.0)
            shares[lev // 4, lev // 2 % 2, lev % 2, t] = value

    mass[0] = summed
    column_copies = [
        remote(mass.at[0], column_in.at[k - 1], t_send.at[k - 1], t_recv.at[k - 1], column_peer(k)) for k in range(1, 8)
    ]
    for copy in column_copies:
        copy.start()
    share_copies = [
        remote(
            shares.at[lax.rem(zone + k, CHUNKS), core], gathered.at[zone], g_send.at[k - 1], g_recv.at[k - 1],
            zone_peer(k),
        )
        for k in (1, 2, 3)
    ]
    for copy in share_copies:
        copy.start()
    gathered[zone] = shares[zone, core]
    for k, copy in enumerate(column_copies):
        copy.wait()
        summed = summed + column_in[k]

    mass[1] = summed

    def plane_copy(k):
        return remote(mass.at[1], plane_in.at[k - 1], p_send.at[k - 1], p_recv.at[k - 1], plane_peer(k))

    def send_plane(k, carry):
        plane_copy(k).start()
        return carry

    lax.fori_loop(1, 32, send_plane, 0)
    for copy in share_copies:
        copy.wait()
    joined = []
    for i in range(2):
        chunks = [[gathered[part, i, t] for t in range(TILES)] for part in range(CHUNKS)]
        joined.append([joined_tile(chunks, index) for index in range(12)])
    for t in range(TILES):
        for k in (1, 2, 3):
            zone_copies[k, t].wait_send()
    rows_sent()
    for copy in far_copies:
        copy.wait_send()

    def take_plane(k, value):
        plane_copy(k).wait()
        return value + plane_in[k - 1]

    summed = lax.fori_loop(1, 32, take_plane, summed)
    cells = LEV * ROWS * lat_count * LON
    scale = cells / jnp.sum(summed)
    for i in range(2):
        for index in range(11):
            out[i, :, pl.ds(128 * index, 128)] = joined[i][index] * scale
        out[i, :, pl.ds(LAST, LON - LAST)] = (joined[i][11] * scale)[:, : LON - LAST]


def local(members, conductivity, weights):
    vmem = functools.partial(pltpu.VMEM, dtype=jnp.float32)
    dma = pltpu.SemaphoreType.DMA
    tiled = (TILES, 8, 128)
    table = (ALL, HALF) + tiled
    return pl.pallas_call(
        kernel,
        name="barycenter",
        out_shape=jax.ShapeDtypeStruct((2, ROWS, LON), jnp.float32),
        in_specs=[
            pl.BlockSpec(memory_space=pl.ANY),
            pl.BlockSpec(memory_space=pl.ANY),
            pl.BlockSpec(memory_space=pltpu.SMEM),
        ],
        out_specs=pl.BlockSpec(memory_space=pltpu.VMEM),
        scratch_shapes=[
            vmem((LEV, ROWS, LON)),
            vmem((LEV, ROWS, LON)),
            vmem((CHUNKS, TILES, HALF, 16, 128)),
            vmem((3, TILES, HALF, 64, 128)),
            vmem((2 * CHUNKS, HALF, 16, 128)),
            vmem((2, TILES, HALF, 8, 128)),
            vmem((3, LEV) + tiled),
            vmem((2, LEV) + tiled),
            vmem(table), vmem(table), vmem(table),
            vmem(table), vmem(table), vmem(table),
            vmem((INNER, 2) + tiled),
            vmem((INNER, 2) + tiled),
            vmem((TILES, 2, 64, 128)),
            vmem((TILES, 2, 64, 128)),
            vmem((CHUNKS, 2, 2) + tiled),
            vmem((CHUNKS, 2) + tiled),
            vmem((8, 128)),
            vmem((3, 8, 128)),
            vmem((8, 128)),
            vmem((8, 128)),
            vmem((2, 8, 128)),
            vmem((7, 8, 128)),
            vmem((31, 8, 128)),
            dma((2,)), dma((3,)), dma((2 * CHUNKS,)),
            dma((3, 3)), dma((3, 3)), dma((3,)), dma((3,)), dma((7,)), dma((7,)),
            dma((4, 3, 2)), dma((4, 3, 2)), dma((4, 2, 2)), dma((4, 2, 2)), dma((4,)), dma((4,)),
            dma((3,)), dma((3,)), dma((7,)), dma((7,)), dma((31,)), dma((31,)),
        ],
        compiler_params=pltpu.CompilerParams(
            collective_id=0, has_side_effects=True, vmem_limit_bytes=60 * 1024 * 1024
        ),
    )(members, conductivity, weights)


def solution(mesh):
    placed = (P("member", None, "lat", None), P(None, "lat", None), P("member"))
    return jax.shard_map(
        local, mesh=mesh, in_specs=placed, out_specs=P("member", "lat", None), check_vma=False
    )
```
